256 devices in a mesh: gx: 32 (over z, x), yz: 8 (over y, core).
Axes of the slice: x: 4, y: 4, z: 8, core: 2. Of those that a mesh axis runs over, the one named last changes fastest.
Arguments:
- state: float32 [3, 256, 256, 256], P(None, 'gx', 'yz'), may hold values from -5 to 5
- direction: float32 [3, 256, 256, 256], P(None, 'gx', 'yz'), may hold values from -16 to 16
- xxt_rows: float32 [8192, 8192], P(('gx', 'yz')), may hold values from -0.0625 to 0.0625
- coarse_ids: int32 [256, 128], P(('gx', 'yz')), may hold values from 0 to 31, as said below
Outputs:
- next_basis: float32 [3, 256, 256, 256], P(None, 'gx', 'yz')
- hessenberg: float32 [2], replicated
The draws below stay inside these ranges and needn't reach their ends.
Inputs may be any that keep to these rules, and one draw needn't show every extreme that they name: `coarse_ids`: each row names its partition's 32 coarse unknowns, each exactly 128 // 32 times.
All inputs are finite; a program needn't handle non-finite values.
Results may differ from the reference program's by a relative error of at most 0.0003.
Values sent between devices are 32-bit elements; how exact they have to be, the bound alone decides.
A program may use at most 128 MiB of HBM per device.

```python
import jax
import jax.numpy as jnp
import numpy as np
from jax import lax

EXD = 1
EYD = 4
EZD = 32
CDEV = 32
EDEV = 128
NPART = 256
NC = 8192
NX = 256
NY = 256
NZ = 256
N_YZ = 8


def draw_direction(key, part):
    full_shape = (3, NX, NY, NZ)
    x_frac = lax.broadcasted_iota(jnp.float32, full_shape, 1) / (NX - 1)
    ramp = jnp.exp(jnp.log(3.0) * x_frac)
    base = jnp.clip(jax.random.normal(key, full_shape, jnp.float32), -4.0, 4.0)
    return base * ramp


def permute_one(subkey):
    return jax.random.permutation(subkey, EDEV)


def draw_coarse_ids(key, part):
    key_list = jax.random.split(key, NPART)
    orders = jax.vmap(permute_one)(key_list)
    return (orders % CDEV).astype(jnp.int32)


def steps_of(stream_key, dims, pieces, smallest, high):
    loudness, own = 1.0, jax.random.fold_in(stream_key, 6)
    for axis_at, blocks in pieces:
        draws = jnp.exp(jax.random.uniform(jax.random.fold_in(own, axis_at), (blocks,), jnp.float32, smallest / len(pieces), high / len(pieces)))
        loudness = loudness * jnp.repeat(draws, dims[axis_at] // blocks).reshape([-1 if axis == axis_at else 1 for axis in range(len(dims))])
    return loudness


def centred(rng, shape, scale, bound, cuts=(), kind=jnp.bfloat16):
    drawn = scale * jax.random.normal(rng, shape, jnp.float32)
    if cuts:
        drawn = drawn * steps_of(rng, shape, cuts, -0.22, 0.18)
    return jnp.clip(drawn, -bound, bound).astype(kind)


def setup_inputs(seed: int = 0) -> dict:
    splits = jax.random.split(jax.random.key(seed), 5)
    return {
        "state": centred(splits[0], (3, NX, NY, NZ), 1.0, 5.0, ((1, 32), (2, 8)), jnp.float32),
        "direction": draw_direction(jax.random.fold_in(splits[4], 71), 0),
        "xxt_rows": centred(splits[2], (NC, NC), NC ** -0.5, 0.0625, ((0, 256),), jnp.float32),
        "coarse_ids": draw_coarse_ids(jax.random.fold_in(splits[4], 71), 0),
    }


viscosity = 0.05
epsilon = 1e-06

def tables():
    points = np.array([-1.0, -0.8717401485096066, -0.5917001814331423, -0.2092992179024789, 0.2092992179024789, 0.5917001814331423, 0.8717401485096066, 1.0])
    weights = np.array([1.0 / 28.0, 0.2107042271435061, 0.3411226924835044, 0.4124587946587038, 0.4124587946587038, 0.3411226924835044, 0.2107042271435061, 1.0 / 28.0])
    differ = points[:, None] - points[None, :]
    positions = np.arange(8)
    differ[positions, positions] = 1.0
    barycentric = 1.0 / np.prod(differ, axis=1)
    derivative = barycentric[None, :] / barycentric[:, None] / differ
    derivative[positions, positions] = 0.0
    derivative[positions, positions] = -derivative.sum(axis=1)
    return (jnp.asarray(derivative, jnp.float32), jnp.asarray(weights, jnp.float32))

def apply_along(tensor, matrix, spatial):
    full_shape = tensor.shape
    blocks = tensor.reshape(full_shape[:spatial] + (full_shape[spatial] // 8, 8) + full_shape[spatial + 1:])
    result = jnp.tensordot(blocks, matrix, axes=((spatial + 1,), (1,)), precision=lax.Precision.HIGHEST)
    result = jnp.moveaxis(result, -1, spatial + 1)
    return result.reshape(full_shape)

def per_point(full_shape, vectors):
    return vectors[0][:, None, None] * vectors[1][None, :, None] * vectors[2][None, None, :]

def mass_field(full_shape, point_w):
    return per_point(full_shape, [jnp.tile(point_w, full_shape[spatial] // 8) for spatial in (1, 2, 3)])

def multiplicity(full_shape):
    vectors = []
    for spatial in (1, 2, 3):
        position = jnp.arange(full_shape[spatial]) % 8
        vectors.append(jnp.where((position == 0) | (position == 7), 0.5, 1.0).astype(jnp.float32))
    return per_point(full_shape, vectors)

def walls_of(full_shape, starts, totals):
    vectors = []
    for spatial in (1, 2, 3):
        global_pos = starts[spatial - 1] + jnp.arange(full_shape[spatial])
        vectors.append(((global_pos > 0) & (global_pos < totals[spatial - 1] - 1)).astype(jnp.float32))
    return per_point(full_shape, vectors)

def fold_dim(tensor, spatial, padded):
    extent = tensor.shape[spatial]
    following = lax.slice_in_dim(padded, 2, extent + 2, axis=spatial)
    before = lax.slice_in_dim(padded, 0, extent, axis=spatial)
    position = lax.broadcasted_iota(jnp.int32, tensor.shape, spatial) % 8
    return tensor + jnp.where(position == 7, following, 0.0) + jnp.where(position == 0, before, 0.0)

def zero_pad(tensor, spatial):
    widths = [(0, 0)] * tensor.ndim
    widths[spatial] = (1, 1)
    return jnp.pad(tensor, widths)

def element_apply(state, state_grads, vector, mass_w, derivative):
    vector_grads = [apply_along(vector, derivative, spatial) for spatial in (1, 2, 3)]
    convect = jnp.zeros_like(vector)
    for spatial in (1, 2, 3):
        convect = convect + state[spatial - 1][None] * vector_grads[spatial - 1] + vector[spatial - 1][None] * state_grads[spatial - 1]
    result = mass_w * convect
    for spatial in (1, 2, 3):
        result = result + viscosity * apply_along(mass_w * vector_grads[spatial - 1], derivative.T, spatial)
    return result

def element_sums(tensor):
    comps, size_a, size_b, size_c = tensor.shape
    return tensor.reshape(comps, size_a // 8, 8, size_b // 8, 8, size_c // 8, 8).sum(axis=(2, 4, 6))

def spread(values):
    return jnp.repeat(jnp.repeat(jnp.repeat(values, 8, axis=1), 8, axis=2), 8, axis=3)

def reference(state, direction, xxt_rows, coarse_ids):
    derivative, point_w = tables()
    full_shape = state.shape
    mass_w = mass_field(full_shape, point_w)
    wall_mask = walls_of(full_shape, (0, 0, 0), full_shape[1:])
    state_grads = [apply_along(state, derivative, spatial) for spatial in (1, 2, 3)]

    def assemble(local_out):
        merged = local_out
        for spatial in (1, 2, 3):
            merged = fold_dim(merged, spatial, zero_pad(merged, spatial))
        return merged * wall_mask
    first_image = assemble(element_apply(state, state_grads, direction, mass_w, derivative))
    totals = element_sums(first_image * mass_w)
    elem_shape = totals.shape[1:]
    elem_x = lax.broadcasted_iota(jnp.int32, elem_shape, 0)
    elem_y = lax.broadcasted_iota(jnp.int32, elem_shape, 1)
    elem_z = lax.broadcasted_iota(jnp.int32, elem_shape, 2)
    owner_dev = elem_x // EXD * N_YZ + elem_y // EYD
    local_slot = (elem_x % EXD * EYD + elem_y % EYD) * EZD + elem_z
    coarse_row = (owner_dev * CDEV + coarse_ids[owner_dev, local_slot]).astype(jnp.int32).reshape(-1)
    coarse_b = jnp.zeros((3, NC), jnp.float32).at[:, coarse_row].add(totals.reshape(3, -1))
    coarse_y = jnp.dot(coarse_b, xxt_rows, precision=lax.Precision.HIGHEST)
    coarse_c = jnp.dot(coarse_y, xxt_rows.T, precision=lax.Precision.HIGHEST)
    correction = coarse_c[:, coarse_row].reshape(totals.shape)
    probe_field = first_image + spread(correction)
    second = assemble(element_apply(state, state_grads, probe_field, mass_w, derivative))
    weight = multiplicity(full_shape)
    weight_total = 343.0 * EDEV * NPART
    proj_mean = jnp.sum(weight * second * probe_field) / weight_total
    probe_mean = jnp.sum(weight * probe_field * probe_field) / weight_total
    projection_coef = proj_mean / (probe_mean + epsilon)
    remainder = second - projection_coef * probe_field
    rest_mean = jnp.sum(weight * remainder * remainder) / weight_total
    rms_scale = jnp.sqrt(rest_mean + epsilon)
    return (remainder / rms_scale, jnp.stack([projection_coef, rms_scale]))
```

```python
import jax
import jax.numpy as jnp
import ml_dtypes
import numpy as np
from jax import lax
from jax.experimental import pallas as pl
from jax.experimental.pallas import tpu as pltpu
from jax.sharding import PartitionSpec as P

viscosity = 0.05
epsilon = 1e-06
MESH = pl.DeviceIdType.MESH
F32 = jnp.float32
BF16 = jnp.bfloat16
PLANE = 32
RING = 8


def tables():
    points = np.array(
        [
            -1.0,
            -0.8717401485096066,
            -0.5917001814331423,
            -0.2092992179024789,
            0.2092992179024789,
            0.5917001814331423,
            0.8717401485096066,
            1.0,
        ]
    )
    weights = np.array(
        [
            1.0 / 28.0,
            0.2107042271435061,
            0.3411226924835044,
            0.4124587946587038,
            0.4124587946587038,
            0.3411226924835044,
            0.2107042271435061,
            1.0 / 28.0,
        ]
    )
    differ = points[:, None] - points[None, :]
    positions = np.arange(8)
    differ[positions, positions] = 1.0
    barycentric = 1.0 / np.prod(differ, axis=1)
    derivative = barycentric[None, :] / barycentric[:, None] / differ
    derivative[positions, positions] = 0.0
    derivative[positions, positions] = -derivative.sum(axis=1)
    return derivative, weights


def halves(matrix):
    high = matrix.astype(ml_dtypes.bfloat16)
    low = (matrix - high.astype(np.float64)).astype(ml_dtypes.bfloat16)
    return high, low


def constants():
    derivative, weights = tables()
    stiff = viscosity * (derivative.T * weights[None, :]) @ derivative / weights[:, None]
    eye = np.eye
    along_x = np.kron(derivative, eye(32))
    along_y = np.kron(eye(32), derivative)
    spread_xy = np.kron(stiff, eye(32)) + np.kron(eye(32), stiff)
    left = np.concatenate([along_x, along_y, spread_xy], axis=0)
    right = np.concatenate([np.kron(eye(32), derivative.T), np.kron(eye(32), stiff.T)], axis=1)
    left = np.concatenate(halves(left), axis=1)
    right = np.concatenate(halves(right), axis=0)
    half = np.where((np.arange(8) == 0) | (np.arange(8) == 7), 0.5, 1.0)
    mass = np.tile(weights, 4)[:, None] * np.tile(weights, 32)[None, :]
    count = np.tile(half, 4)[:, None] * np.tile(half, 32)[None, :]
    return left, right, np.stack([mass, count]).astype(np.float32), weights


WEIGHTS = tables()[1]


def split(value):
    high = value.astype(BF16)
    return high, (value - high.astype(F32)).astype(BF16)


def kernel(
    slabs,
    columns,
    state_hbm,
    dir_hbm,
    xxt_hbm,
    ids_hbm,
    left_hbm,
    right_hbm,
    plane_hbm,
    sec_hbm,
    probe_hbm,
    scal_ref,
    state,
    direc,
    xxt,
    ids,
    left,
    right,
    plane,
    grads,
    lhs_out,
    rhs_out,
    local,
    image,
    local2,
    second,
    probe,
    onehot,
    cblock,
    part_y,
    recv_y,
    sum_b,
    recv_b,
    all_y,
    send_yl,
    send_yh,
    send_c,
    recv_xl,
    recv_xh,
    recv_yl,
    recv_yh,
    recv_c,
    row_a,
    recv_ra,
    row_b,
    recv_rb,
    in_sem,
    out_sem,
    halo_send,
    halo_recv,
    red_send,
    red_recv,
):
    gx, yz = lax.axis_index("gx"), lax.axis_index("yz")
    gz, px = gx // 4, gx % 4
    here = px * columns + yz

    def in_plane(k):
        other = lax.rem(here + k, PLANE)
        return (gz * 4 + other // columns, lax.rem(other, columns))

    def in_ring(k):
        return (lax.rem(gz + k, RING) * 4 + px, yz)

    def beside(dx, dy):
        return (lax.rem(gx + dx + slabs, slabs), lax.rem(yz + dy + columns, columns))

    loads = [
        pltpu.make_async_copy(src, dst, in_sem.at[i])
        for i, (src, dst) in enumerate(
            [
                (state_hbm, state),
                (left_hbm, left),
                (right_hbm, right),
                (dir_hbm, direc),
                (plane_hbm, plane),
                (ids_hbm, ids),
                (xxt_hbm, xxt),
            ]
        )
    ]
    for load in loads:
        load.start()

    barrier = pltpu.get_barrier_semaphore()
    greeted = [in_plane(k) for k in range(1, PLANE)]
    greeted += [in_ring(k) for k in range(1, RING)]
    greeted += [beside(dx, dy) for dx in (-1, 1) for dy in (-1, 0, 1)]
    for peer in greeted:
        pl.semaphore_signal(barrier, inc=1, device_id=peer, device_id_type=MESH)

    lane = lax.broadcasted_iota(jnp.int32, (1, 256), 1)
    from_next = ((lane % 8 == 7) & (lane != 255)).astype(F32)
    from_last = ((lane % 8 == 0) & (lane != 0)).astype(F32)
    inside = ((lane != 0) & (lane != 255)).astype(F32)
    wall_xl = jnp.where(gx == 0, 0.0, 1.0).astype(F32)
    wall_xh = jnp.where(gx == slabs - 1, 0.0, 1.0).astype(F32)
    wall_yl = jnp.where(yz == 0, 0.0, 1.0).astype(F32)
    wall_yh = jnp.where(yz == columns - 1, 0.0, 1.0).astype(F32)
    row8 = lax.broadcasted_iota(jnp.int32, (8, 1), 0)
    wall_x = jnp.where(row8 == 0, wall_xl, jnp.where(row8 == 7, wall_xh, 1.0))

    def fold_z(value):
        return (
            value * inside
            + pltpu.roll(value, 255, 1) * from_next
            + pltpu.roll(value, 1, 1) * from_last
        )

    def rows_of(p):
        return pl.ds(32 * p, 32)

    def get(ref, m, rows):
        return jnp.concatenate([ref[m, 0, rows, :], ref[m, 1, rows, :]], axis=1)

    def put(ref, m, rows, value):
        ref[m, 0, rows, :] = value[:, :128]
        ref[m, 1, rows, :] = value[:, 128:]

    def whole(ref, m, rows):
        return ref[m, rows, :]

    def products_left(value, rows, slot):
        high, low = split(value)
        ops = left[pl.ds(0, rows), :]
        lhs_out[slot, pl.ds(0, rows), :] = jnp.dot(
            jnp.concatenate([ops, ops[:, :256]], axis=1),
            jnp.concatenate([high, high, low], axis=0),
            preferred_element_type=F32,
        )
        return high, low

    def products_right(high, low, cols):
        ops = right[:, pl.ds(0, cols)]
        return jnp.dot(
            jnp.concatenate([high, high, low], axis=1),
            jnp.concatenate([ops, ops[:256]], axis=0),
            preferred_element_type=F32,
        )

    def apply_element(vector, take, m, target, slot):
        high, low = products_left(take(vector, m, pl.ds(0, 256)), 768, slot)
        rhs_out[slot] = products_right(high, low, 512)
        for p in (0, 7, 1, 2, 3, 4, 5, 6):
            rows = rows_of(p)
            total = lhs_out[slot, pl.ds(512 + 32 * p, 32), :] + rhs_out[slot, rows, pl.ds(256, 256)]
            total += state[0, rows, :] * lhs_out[slot, rows, :]
            total += state[1, rows, :] * lhs_out[slot, pl.ds(256 + 32 * p, 32), :]
            total += state[2, rows, :] * rhs_out[slot, rows, pl.ds(0, 256)]
            for k in range(3):
                total += take(vector, k, rows) * grads[m, k, rows, :]
            put(target, m, rows, total * (plane[0] * float(WEIGHTS[p])))

    def send(turn, index, src, dst, peer):
        pltpu.make_async_remote_copy(
            src_ref=src,
            dst_ref=dst,
            send_sem=halo_send.at[turn, index],
            recv_sem=halo_recv.at[turn, index],
            device_id=peer,
            device_id_type=MESH,
        ).start()

    def send_x(turn, source, m):
        send(turn, 0, source.at[m, :, pl.ds(224, 32), :], recv_xl.at[turn, m], beside(1, 0))
        send(turn, 1, source.at[m, :, pl.ds(0, 32), :], recv_xh.at[turn, m], beside(-1, 0))

    def send_y(turn, source):
        for m in range(3):
            low = get(source, m, pl.ds(0, 8, stride=32))
            high = get(source, m, pl.ds(31, 8, stride=32))
            send_yl[turn, m] = low
            send_yh[turn, m] = high
            send_c[turn, 0, pl.ds(m, 1), :] = low[0:1]
            send_c[turn, 1, pl.ds(m, 1), :] = high[0:1]
            send_c[turn, 2, pl.ds(m, 1), :] = low[7:8]
            send_c[turn, 3, pl.ds(m, 1), :] = high[7:8]
        send(turn, 2, send_yh.at[turn], recv_yl.at[turn], beside(0, 1))
        send(turn, 3, send_yl.at[turn], recv_yh.at[turn], beside(0, -1))
        for i, (dx, dy) in enumerate(((-1, -1), (-1, 1), (1, -1), (1, 1))):
            send(turn, 4 + i, send_c.at[turn, i], recv_c.at[turn, i], beside(dx, dy))

    def halo_refs(turn):
        refs = [recv_xl.at[turn], recv_xh.at[turn], recv_yl.at[turn], recv_yh.at[turn]]
        return refs + [recv_c.at[turn, i] for i in range(4)]

    def wait_halo(turn, sems):
        for i, ref in enumerate(halo_refs(turn)):
            pltpu.make_async_copy(ref, ref, sems.at[turn, i]).wait()

    def assemble(turn, source, target):
        for m in range(3):
            for p in range(8):
                value = get(source, m, rows_of(p))
                if p == 0:
                    value = (value + get(recv_xl.at[turn], m, pl.ds(0, 32))) * wall_xl
                if p == 7:
                    value = (value + get(recv_xh.at[turn], m, pl.ds(0, 32))) * wall_xh
                put(target, m, rows_of(p), fold_z(value))
            at_m = pl.ds(m, 1)
            low = recv_yl[turn, m]
            low += jnp.where(row8 == 0, recv_c[turn, 3, at_m, :], 0.0)
            low += jnp.where(row8 == 7, recv_c[turn, 1, at_m, :], 0.0)
            high = recv_yh[turn, m]
            high += jnp.where(row8 == 0, recv_c[turn, 2, at_m, :], 0.0)
            high += jnp.where(row8 == 7, recv_c[turn, 0, at_m, :], 0.0)
            first, last = pl.ds(0, 8, stride=32), pl.ds(31, 8, stride=32)
            put(target, m, first, (get(target, m, first) + fold_z(low) * wall_x) * wall_yl)
            put(target, m, last, (get(target, m, last) + fold_z(high) * wall_x) * wall_yh)
            for b in range(3):
                one, two = pl.ds(8 * b + 7, 8, stride=32), pl.ds(8 * b + 8, 8, stride=32)
                both = get(target, m, one) + get(target, m, two)
                put(target, m, one, both)
                put(target, m, two, both)

    def spread_out(phase, size, peer_of, src_of, dst_of):
        for k in range(1, size):
            pltpu.make_async_remote_copy(
                src_ref=src_of(k),
                dst_ref=dst_of(k),
                send_sem=red_send.at[phase],
                recv_sem=red_recv.at[phase],
                device_id=peer_of(k),
                device_id_type=MESH,
            ).start()

    def wait_bytes(ref, sem):
        pltpu.make_async_copy(ref, ref, sem).wait()

    loads[0].wait()
    loads[1].wait()
    loads[2].wait()
    loads[3].wait()
    loads[4].wait()
    for m in range(3):
        slot = m % 2
        high, low = products_left(state[m], 512, slot)
        grads[m, 2] = products_right(high, low, 256)
        grads[m, 0] = lhs_out[slot, pl.ds(0, 256), :]
        grads[m, 1] = lhs_out[slot, pl.ds(256, 256), :]
    for m in range(3):
        apply_element(direc, whole, m, local, m % 2)
        if m == 0:
            pl.semaphore_wait(barrier, len(greeted))
        send_x(0, local, m)
    send_y(0, local)

    loads[5].wait()
    elem = lax.broadcasted_iota(jnp.int32, (128, 1024), 0)
    spot = lax.broadcasted_iota(jnp.int32, (128, 1024), 1)
    wide = jnp.dot(
        jnp.broadcast_to(ids[...].astype(F32), (8, 128)).astype(BF16),
        (spot // 8 == elem).astype(F32).astype(BF16),
        preferred_element_type=F32,
    )
    for t in range(4):
        row = (lax.broadcasted_iota(jnp.int32, (8, 1024), 0) + 8 * t).astype(F32)
        onehot[pl.ds(8 * t, 8), :] = jnp.where(jnp.abs(wide - row) < 0.5, 1.0, 0.0)
    loads[6].wait()

    wait_halo(0, halo_recv)
    assemble(0, local, image)

    coarse = []
    for m in range(3):
        total = get(image, m, rows_of(0)) * float(WEIGHTS[0])
        for p in range(1, 8):
            total += get(image, m, rows_of(p)) * float(WEIGHTS[p])
        total *= plane[0]
        acc = jnp.zeros((32, 256), F32)
        for b in range(4):
            line = jnp.sum(total[8 * b : 8 * b + 8], axis=0, keepdims=True)
            acc += onehot[:, pl.ds(256 * b, 256)] * line
        coarse.append(jnp.sum(acc, axis=1, keepdims=True))
    for j in range(PLANE):
        block = xxt[:, pl.ds(256 * j, 256)]
        for m in range(3):
            part_y[j, pl.ds(m, 1), :] = jnp.sum(block * coarse[m], axis=0, keepdims=True)

    spread_out(
        0,
        PLANE,
        in_plane,
        lambda k: part_y.at[lax.rem(here + k, PLANE)],
        lambda k: recv_y.at[k - 1],
    )
    apply_element(image, get, 0, local2, 0)
    wait_bytes(recv_y, red_recv.at[0])
    total = part_y[here]
    for k in range(PLANE - 1):
        total += recv_y[k]
    sum_b[...] = total
    spread_out(1, RING, in_ring, lambda k: sum_b, lambda k: recv_b.at[k - 1])
    apply_element(image, get, 1, local2, 1)
    wait_bytes(recv_b, red_recv.at[1])
    total = sum_b[...]
    for k in range(RING - 1):
        total += recv_b[k]
    all_y[here] = total
    spread_out(2, PLANE, in_plane, lambda k: all_y.at[here], lambda k: all_y.at[here])
    apply_element(image, get, 2, local2, 0)
    wait_bytes(all_y.at[pl.ds(0, PLANE - 1)], red_recv.at[2])

    sums = [jnp.zeros((32, 256), F32) for _ in range(3)]
    for j in range(PLANE):
        block = xxt[:, pl.ds(256 * j, 256)]
        for m in range(3):
            sums[m] += block * all_y[j, pl.ds(m, 1), :]
    for m in range(3):
        column = jnp.sum(sums[m], axis=1, keepdims=True)
        for b in range(4):
            line = jnp.sum(onehot[:, pl.ds(256 * b, 256)] * column, axis=0, keepdims=True)
            cblock[m, pl.ds(8 * b, 8), :] = jnp.broadcast_to(line, (8, 256))

    def add_correction(m, p):
        rows = rows_of(p)
        total = cblock[0] * grads[m, 0, rows, :]
        total += cblock[1] * grads[m, 1, rows, :]
        total += cblock[2] * grads[m, 2, rows, :]
        put(local2, m, rows, get(local2, m, rows) + total * (plane[0] * float(WEIGHTS[p])))

    for m in range(3):
        add_correction(m, 0)
        add_correction(m, 7)
        send_x(1, local2, m)
    for m in range(3):
        for p in range(1, 7):
            add_correction(m, p)
    send_y(1, local2)
    for m in range(3):
        for p in range(8):
            probe[m, rows_of(p), :] = get(image, m, rows_of(p)) + cblock[m]
    probe_out = pltpu.make_async_copy(probe, probe_hbm, out_sem.at[0])
    probe_out.start()
    wait_halo(1, halo_recv)
    assemble(1, local2, second)
    second_out = [
        pltpu.make_async_copy(
            second.at[:, h], sec_hbm.at[:, :, pl.ds(128 * h, 128)], out_sem.at[1 + h]
        )
        for h in range(2)
    ]
    for out in second_out:
        out.start()

    def both_sums(one, two):
        results = []
        for value in (one, two):
            results.append(jnp.sum(jnp.sum(value * plane[1], axis=0, keepdims=True), axis=1, keepdims=True))
        return results

    acc_sp, acc_pp = jnp.zeros((32, 256), F32), jnp.zeros((32, 256), F32)
    for p in range(8):
        sp, pp = jnp.zeros((32, 256), F32), jnp.zeros((32, 256), F32)
        for m in range(3):
            pr = probe[m, rows_of(p), :]
            sp += get(second, m, rows_of(p)) * pr
            pp += pr * pr
        scale = 0.5 if p in (0, 7) else 1.0
        acc_sp += scale * sp
        acc_pp += scale * pp
    sp, pp = both_sums(acc_sp, acc_pp)
    own = jnp.where(pp > 0, sp / jnp.where(pp > 0, pp, 1.0), 0.0)
    acc_q, acc_rr = jnp.zeros((32, 256), F32), jnp.zeros((32, 256), F32)
    for p in range(8):
        q, rr = jnp.zeros((32, 256), F32), jnp.zeros((32, 256), F32)
        for m in range(3):
            pr = probe[m, rows_of(p), :]
            rest = get(second, m, rows_of(p)) - own * pr
            q += rest * pr
            rr += rest * rest
        scale = 0.5 if p in (0, 7) else 1.0
        acc_q += scale * q
        acc_rr += scale * rr
    q, rr = both_sums(acc_q, acc_rr)

    lane128 = lax.broadcasted_iota(jnp.int32, (1, 128), 1)

    def pack(one, two, three, four):
        rest = jnp.where(lane128 < 96, three, four)
        return jnp.where(lane128 < 32, one, jnp.where(lane128 < 64, two, rest))

    def unpack(rows):
        return rows, pltpu.roll(rows, 96, 1), pltpu.roll(rows, 64, 1), pltpu.roll(rows, 32, 1)

    def total_of(rows):
        return jnp.sum(rows, axis=0, keepdims=True)

    def gather_rows(own_row, ref, count):
        return jnp.concatenate([own_row] + [ref[k] for k in range(count)], axis=0)

    message = pack(own, q, pp, rr)
    row_a[...] = message
    spread_out(3, PLANE, in_plane, lambda k: row_a, lambda k: recv_ra.at[k - 1])
    wait_bytes(recv_ra, red_recv.at[3])
    own, q, pp, rr = unpack(gather_rows(message, recv_ra, PLANE - 1))
    mean_sp, mean_pp = total_of(q + own * pp), total_of(pp)
    merged = jnp.where(mean_pp > 0, mean_sp / jnp.where(mean_pp > 0, mean_pp, 1.0), 0.0)
    away = own - merged
    q, rr = total_of(q + away * pp), total_of(rr + 2.0 * away * q + away * away * pp)
    message = pack(merged, pltpu.roll(q, 32, 1), pltpu.roll(mean_pp, 64, 1), pltpu.roll(rr, 96, 1))
    row_b[...] = message
    spread_out(4, RING, in_ring, lambda k: row_b, lambda k: recv_rb.at[k - 1])
    wait_bytes(recv_rb, red_recv.at[4])
    own, q, pp, rr = unpack(gather_rows(message, recv_rb, RING - 1))
    weight_total = 343.0 * 128 * slabs * columns
    mean_sp, mean_pp = total_of(q + own * pp) / weight_total, total_of(pp) / weight_total
    coef = mean_sp / (mean_pp + epsilon)
    away = own - coef
    rest_mean = total_of(rr + 2.0 * away * q + away * away * pp) / weight_total
    rms = jnp.sqrt(jnp.maximum(rest_mean, 0.0) + epsilon)
    scal_ref[...] = jnp.concatenate([coef, rms, 1.0 / rms, jnp.zeros((5, 128), F32)], axis=0)

    wait_halo(0, halo_send)
    wait_halo(1, halo_send)
    wait_bytes(recv_y, red_send.at[0])
    wait_bytes(recv_b, red_send.at[1])
    wait_bytes(all_y.at[pl.ds(0, PLANE - 1)], red_send.at[2])
    wait_bytes(recv_ra, red_send.at[3])
    wait_bytes(recv_rb, red_send.at[4])
    probe_out.wait()
    for out in second_out:
        out.wait()


def shards(slabs, columns, state, direction, xxt_rows, coarse_ids):
    shape = state.shape
    left, right, plane, _ = constants()
    vmem = pltpu.VMEM
    field = (3, 256, 256)
    halved = (3, 2, 256, 128)

    def body(*refs):
        kernel(slabs, columns, *refs)

    anywhere = pl.BlockSpec(memory_space=pl.ANY)
    sec, probe, scal = pl.pallas_call(
        body,
        out_shape=(
            jax.ShapeDtypeStruct(field, F32),
            jax.ShapeDtypeStruct(field, F32),
            jax.ShapeDtypeStruct((8, 128), F32),
        ),
        in_specs=[anywhere] * 7,
        out_specs=(anywhere, anywhere, pl.BlockSpec(memory_space=vmem)),
        scratch_shapes=[
            vmem(field, F32),
            vmem(field, F32),
            vmem((32, 8192), F32),
            vmem((1, 128), jnp.int32),
            vmem((768, 512), BF16),
            vmem((512, 512), BF16),
            vmem((2, 32, 256), F32),
            vmem((3, 3, 256, 256), F32),
            vmem((2, 768, 256), F32),
            vmem((2, 256, 512), F32),
            vmem(halved, F32),
            vmem(halved, F32),
            vmem(halved, F32),
            vmem(halved, F32),
            vmem(field, F32),
            vmem((32, 1024), F32),
            vmem((3, 32, 256), F32),
            vmem((PLANE, 4, 256), F32),
            vmem((PLANE - 1, 4, 256), F32),
            vmem((4, 256), F32),
            vmem((RING - 1, 4, 256), F32),
            vmem((PLANE, 4, 256), F32),
            vmem((2, 3, 8, 256), F32),
            vmem((2, 3, 8, 256), F32),
            vmem((2, 4, 4, 256), F32),
            vmem((2, 3, 2, 32, 128), F32),
            vmem((2, 3, 2, 32, 128), F32),
            vmem((2, 3, 8, 256), F32),
            vmem((2, 3, 8, 256), F32),
            vmem((2, 4, 4, 256), F32),
            vmem((1, 128), F32),
            vmem((PLANE - 1, 1, 128), F32),
            vmem((1, 128), F32),
            vmem((RING - 1, 1, 128), F32),
            pltpu.SemaphoreType.DMA((7,)),
            pltpu.SemaphoreType.DMA((3,)),
            pltpu.SemaphoreType.DMA((2, 8)),
            pltpu.SemaphoreType.DMA((2, 8)),
            pltpu.SemaphoreType.DMA((5,)),
            pltpu.SemaphoreType.DMA((5,)),
        ],
        compiler_params=pltpu.CompilerParams(
            collective_id=0, has_side_effects=True, vmem_limit_bytes=40 * 1024 * 1024
        ),
        name="jacobian_products",
    )(
        state.reshape(field),
        direction.reshape(field),
        xxt_rows,
        coarse_ids,
        jnp.asarray(left),
        jnp.asarray(right),
        jnp.asarray(plane),
    )
    next_basis = (sec - scal[0, 0] * probe) * scal[2, 0]
    return next_basis.reshape(shape), scal[:2, 0]


def solution(mesh):
    slabs, columns = mesh.shape["gx"], mesh.shape["yz"]

    def local_shards(*args):
        return shards(slabs, columns, *args)

    return jax.shard_map(
        local_shards,
        mesh=mesh,
        in_specs=(
            P(None, "gx", "yz", None),
            P(None, "gx", "yz", None),
            P(("gx", "yz"), None),
            P(("gx", "yz"), None),
        ),
        out_specs=(P(None, "gx", "yz", None), P()),
        check_vma=False,
    )
```

```python
import jax
import jax.numpy as jnp
import ml_dtypes
import numpy as np
from jax import lax
from jax.experimental import pallas as pl
from jax.experimental.pallas import tpu as pltpu
from jax.sharding import PartitionSpec as P

viscosity = 0.05
epsilon = 1e-06
MESH = pl.DeviceIdType.MESH
F32 = jnp.float32
BF16 = jnp.bfloat16
PLANE = 32
RING = 8
VMEM_LIMIT = 60 * 1024 * 1024


def tables():
    points = np.array(
        [
            -1.0,
            -0.8717401485096066,
            -0.5917001814331423,
            -0.2092992179024789,
            0.2092992179024789,
            0.5917001814331423,
            0.8717401485096066,
            1.0,
        ]
    )
    weights = np.array(
        [
            1.0 / 28.0,
            0.2107042271435061,
            0.3411226924835044,
            0.4124587946587038,
            0.4124587946587038,
            0.3411226924835044,
            0.2107042271435061,
            1.0 / 28.0,
        ]
    )
    differ = points[:, None] - points[None, :]
    positions = np.arange(8)
    differ[positions, positions] = 1.0
    barycentric = 1.0 / np.prod(differ, axis=1)
    derivative = barycentric[None, :] / barycentric[:, None] / differ
    derivative[positions, positions] = 0.0
    derivative[positions, positions] = -derivative.sum(axis=1)
    return derivative, weights


GROUPS = ((0, 64, (0, 7)), (192, 192, (1, 2, 3, 4, 5, 6)))
DIMS = {"z": 8, "x": 4, "y": 4, "c": 2}


def offsets(names):
    found = []
    for k in range(1, int(np.prod([DIMS[n] for n in names]))):
        place, hops, rest = {}, 0.0, k
        for n in reversed(names):
            place[n] = rest % DIMS[n]
            rest //= DIMS[n]
            near = min(place[n], DIMS[n] - place[n])
            hops += 0.25 * near if n == "c" else near
        found.append((-hops, k, place))
    return [(k, place) for _, k, place in sorted(found, key=lambda item: item[:2])]


def halves(matrix):
    high = matrix.astype(ml_dtypes.bfloat16)
    low = (matrix - high.astype(np.float64)).astype(ml_dtypes.bfloat16)
    return high, low


def constants():
    derivative, weights = tables()
    stiff = viscosity * (derivative.T * weights[None, :]) @ derivative / weights[:, None]
    eye = np.eye
    along_x = np.kron(derivative, eye(32))
    along_y = np.kron(eye(32), derivative)
    spread_xy = np.kron(stiff, eye(32)) + np.kron(eye(32), stiff)
    left = [
        op[32 * plane : 32 * plane + 32]
        for _, _, planes in GROUPS
        for op in (along_x, along_y, spread_xy)
        for plane in planes
    ]
    left = np.concatenate(left, axis=0)
    right = np.concatenate([np.kron(eye(32), derivative.T), np.kron(eye(32), stiff.T)], axis=1)
    left = np.concatenate(halves(left), axis=1)
    right = np.concatenate(halves(right), axis=0)
    half = np.where((np.arange(8) == 0) | (np.arange(8) == 7), 0.5, 1.0)
    mass = np.tile(weights, 4)[:, None] * np.tile(weights, 32)[None, :]
    count = np.tile(half, 4)[:, None] * np.tile(half, 32)[None, :]
    return left, right, np.stack([mass, count]).astype(np.float32), weights


WEIGHTS = tables()[1]


def split(value):
    high = value.astype(BF16)
    return high, (value - high.astype(F32)).astype(BF16)


def kernel(
    slabs,
    columns,
    state_hbm,
    dir_hbm,
    xxt_hbm,
    ids_hbm,
    left_hbm,
    right_hbm,
    plane_hbm,
    sec_hbm,
    probe_hbm,
    scal_ref,
    state,
    direc,
    xxt,
    ids,
    left,
    right,
    plane,
    highs,
    lows,
    grads,
    lhs_out,
    rhs_out,
    local,
    image,
    local2,
    second,
    probe,
    onehot,
    cblock,
    part_y,
    recv_y,
    sum_b,
    recv_b,
    all_y,
    send_yl,
    send_yh,
    send_c,
    recv_xl,
    recv_xh,
    recv_yl,
    recv_yh,
    recv_c,
    row_a,
    recv_ra,
    in_sem,
    out_sem,
    halo_send,
    halo_recv,
    red_send,
    red_recv,
):
    gx, yz = lax.axis_index("gx"), lax.axis_index("yz")
    gz, px = gx // 4, gx % 4
    here = px * columns + yz

    def peer_at(place):
        z = lax.rem(gz + place.get("z", 0), 8)
        x = lax.rem(px + place.get("x", 0), 4)
        y = lax.rem(yz // 2 + place.get("y", 0), 4)
        c = lax.rem(yz % 2 + place.get("c", 0), 2)
        return (z * 4 + x, y * 2 + c)

    in_plane, in_ring, everyone = offsets("xyc"), offsets("z"), offsets("zxyc")

    def beside(dx, dy):
        return (lax.rem(gx + dx + slabs, slabs), lax.rem(yz + dy + columns, columns))

    pairs = [(left_hbm, left), (state_hbm.at[0], state.at[0]), (right_hbm, right)]
    pairs += [(state_hbm.at[m], state.at[m]) for m in (1, 2)]
    pairs += [(dir_hbm.at[m], direc.at[m]) for m in range(3)]
    pairs += [(plane_hbm, plane), (ids_hbm, ids), (xxt_hbm, xxt)]
    loads = [pltpu.make_async_copy(src, dst, in_sem.at[i]) for i, (src, dst) in enumerate(pairs)]
    for load in loads[:-1]:
        load.start()

    barrier = pltpu.get_barrier_semaphore()
    greeted = [peer_at(place) for _, place in in_plane + in_ring]
    greeted += [beside(dx, dy) for dx in (-1, 1) for dy in (-1, 0, 1)]
    for peer in greeted:
        pl.semaphore_signal(barrier, inc=1, device_id=peer, device_id_type=MESH)

    lane = lax.broadcasted_iota(jnp.int32, (1, 256), 1)
    from_next = ((lane % 8 == 7) & (lane != 255)).astype(F32)
    from_last = ((lane % 8 == 0) & (lane != 0)).astype(F32)
    inside = ((lane != 0) & (lane != 255)).astype(F32)
    wall_xl = jnp.where(gx == 0, 0.0, 1.0).astype(F32)
    wall_xh = jnp.where(gx == slabs - 1, 0.0, 1.0).astype(F32)
    wall_yl = jnp.where(yz == 0, 0.0, 1.0).astype(F32)
    wall_yh = jnp.where(yz == columns - 1, 0.0, 1.0).astype(F32)
    row8 = lax.broadcasted_iota(jnp.int32, (8, 1), 0)
    wall_x = jnp.where(row8 == 0, wall_xl, jnp.where(row8 == 7, wall_xh, 1.0))

    def fold_z(value):
        return (
            value * inside
            + pltpu.roll(value, 255, 1) * from_next
            + pltpu.roll(value, 1, 1) * from_last
        )

    def rows_of(p):
        return pl.ds(32 * p, 32)

    def get(ref, m, rows):
        return jnp.concatenate([ref[m, 0, rows, :], ref[m, 1, rows, :]], axis=1)

    def put(ref, m, rows, value):
        ref[m, 0, rows, :] = value[:, :128]
        ref[m, 1, rows, :] = value[:, 128:]

    def whole(ref, m, rows):
        return ref[m, rows, :]

    def split_into(value, which, m):
        high, low = split(value)
        highs[which, m] = high
        lows[which, m] = low

    def products_left(which, m, g, count):
        first, rows, _ = GROUPS[g]
        ops = left[pl.ds(first, rows * count), :]
        high, low = highs[which, m], lows[which, m]
        return jnp.dot(
            jnp.concatenate([ops, ops[:, :256]], axis=1),
            jnp.concatenate([high, high, low], axis=0),
            preferred_element_type=F32,
        )

    def products_right(which, m, g, cols):
        ops = right[:, pl.ds(0, cols)]
        high, low = (
            jnp.concatenate([ref[which, m, rows_of(p), :] for p in GROUPS[g][2]], axis=0)
            for ref in (highs, lows)
        )
        return jnp.dot(
            jnp.concatenate([high, high, low], axis=1),
            jnp.concatenate([ops, ops[:256]], axis=0),
            preferred_element_type=F32,
        )

    def state_gradients(m, g):
        _, size, planes = GROUPS[g]
        by_left = products_left(0, m, g, 2)
        by_right = products_right(0, m, g, 256)
        for i, p in enumerate(planes):
            grads[m, 0, rows_of(p), :] = by_left[32 * i : 32 * i + 32]
            grads[m, 1, rows_of(p), :] = by_left[size + 32 * i : size + 32 * i + 32]
            grads[m, 2, rows_of(p), :] = by_right[32 * i : 32 * i + 32]

    def multiply(which, m, g):
        first, size, planes = GROUPS[g]
        lhs_out[m, pl.ds(first, 3 * size), :] = products_left(which, m, g, 3)
        by_right = products_right(which, m, g, 512)
        for i, p in enumerate(planes):
            rhs_out[m, rows_of(p), :] = by_right[32 * i : 32 * i + 32]

    def combine(vector, take, m, g, target):
        first, size, planes = GROUPS[g]
        for i, p in enumerate(planes):
            rows = rows_of(p)
            at = [pl.ds(first + size * op + 32 * i, 32) for op in range(3)]
            total = lhs_out[m, at[2], :] + rhs_out[m, rows, pl.ds(256, 256)]
            total += state[0, rows, :] * lhs_out[m, at[0], :]
            total += state[1, rows, :] * lhs_out[m, at[1], :]
            total += state[2, rows, :] * rhs_out[m, rows, pl.ds(0, 256)]
            for k in range(3):
                total += take(vector, k, rows) * grads[m, k, rows, :]
            put(target, m, rows, total * (plane[0] * float(WEIGHTS[p])))

    def apply_to_image(m):
        split_into(get(image, m, pl.ds(0, 256)), 1, m)
        for g in range(2):
            multiply(1, m, g)
            combine(image, get, m, g, local2)

    def send(turn, index, src, dst, peer):
        pltpu.make_async_remote_copy(
            src_ref=src,
            dst_ref=dst,
            send_sem=halo_send.at[turn, index],
            recv_sem=halo_recv.at[turn, index],
            device_id=peer,
            device_id_type=MESH,
        ).start()

    def send_x(turn, source, m):
        send(turn, 0, source.at[m, :, pl.ds(224, 32), :], recv_xl.at[turn, m], beside(1, 0))
        send(turn, 1, source.at[m, :, pl.ds(0, 32), :], recv_xh.at[turn, m], beside(-1, 0))

    def send_y(turn, source):
        for m in range(3):
            low = get(source, m, pl.ds(0, 8, stride=32))
            high = get(source, m, pl.ds(31, 8, stride=32))
            send_yl[turn, m] = low
            send_yh[turn, m] = high
            send_c[turn, 0, pl.ds(m, 1), :] = low[0:1]
            send_c[turn, 1, pl.ds(m, 1), :] = high[0:1]
            send_c[turn, 2, pl.ds(m, 1), :] = low[7:8]
            send_c[turn, 3, pl.ds(m, 1), :] = high[7:8]
        send(turn, 2, send_yh.at[turn], recv_yl.at[turn], beside(0, 1))
        send(turn, 3, send_yl.at[turn], recv_yh.at[turn], beside(0, -1))
        for i, (dx, dy) in enumerate(((-1, -1), (-1, 1), (1, -1), (1, 1))):
            send(turn, 4 + i, send_c.at[turn, i], recv_c.at[turn, i], beside(dx, dy))

    def halo_refs(turn):
        refs = [recv_xl.at[turn], recv_xh.at[turn], recv_yl.at[turn], recv_yh.at[turn]]
        return refs + [recv_c.at[turn, i] for i in range(4)]

    def wait_halo(turn, sems):
        for i, ref in enumerate(halo_refs(turn)):
            pltpu.make_async_copy(ref, ref, sems.at[turn, i]).wait()

    def assemble_inside(source, target):
        for m in range(3):
            for p in range(1, 7):
                put(target, m, rows_of(p), fold_z(get(source, m, rows_of(p))))

    def assemble_faces(turn, source, target):
        for m in range(3):
            value = get(source, m, rows_of(0)) + get(recv_xl.at[turn], m, pl.ds(0, 32))
            put(target, m, rows_of(0), fold_z(value * wall_xl))
            value = get(source, m, rows_of(7)) + get(recv_xh.at[turn], m, pl.ds(0, 32))
            put(target, m, rows_of(7), fold_z(value * wall_xh))
            at_m = pl.ds(m, 1)
            low = recv_yl[turn, m]
            low += jnp.where(row8 == 0, recv_c[turn, 3, at_m, :], 0.0)
            low += jnp.where(row8 == 7, recv_c[turn, 1, at_m, :], 0.0)
            high = recv_yh[turn, m]
            high += jnp.where(row8 == 0, recv_c[turn, 2, at_m, :], 0.0)
            high += jnp.where(row8 == 7, recv_c[turn, 0, at_m, :], 0.0)
            first, last = pl.ds(0, 8, stride=32), pl.ds(31, 8, stride=32)
            put(target, m, first, (get(target, m, first) + fold_z(low) * wall_x) * wall_yl)
            put(target, m, last, (get(target, m, last) + fold_z(high) * wall_x) * wall_yh)
            for b in range(3):
                one, two = pl.ds(8 * b + 7, 8, stride=32), pl.ds(8 * b + 8, 8, stride=32)
                both = get(target, m, one) + get(target, m, two)
                put(target, m, one, both)
                put(target, m, two, both)

    def spread_out(phase, places, src_of, dst_of):
        for k, place in places:
            peer = peer_at(place)
            pltpu.make_async_remote_copy(
                src_ref=src_of(peer),
                dst_ref=dst_of(k),
                send_sem=red_send.at[phase],
                recv_sem=red_recv.at[phase],
                device_id=peer,
                device_id_type=MESH,
            ).start()

    def wait_bytes(ref, sem):
        pltpu.make_async_copy(ref, ref, sem).wait()

    loads[0].wait()
    for m in range(3):
        loads[(1, 3, 4)[m]].wait()
        split_into(state[m], 0, m)
        if m == 0:
            loads[2].wait()
        state_gradients(m, 0)
    for m in range(3):
        loads[5 + m].wait()
        split_into(direc[m], 1, m)
        multiply(1, m, 0)
    loads[8].wait()
    for m in range(3):
        combine(direc, whole, m, 0, local)
        if m == 0:
            pl.semaphore_wait(barrier, len(greeted))
        send_x(0, local, m)
    loads[10].start()
    for m in range(3):
        state_gradients(m, 1)
        multiply(1, m, 1)
        combine(direc, whole, m, 1, local)
    send_y(0, local)
    assemble_inside(local, image)

    loads[9].wait()
    elem = lax.broadcasted_iota(jnp.int32, (128, 1024), 0)
    spot = lax.broadcasted_iota(jnp.int32, (128, 1024), 1)
    wide = jnp.dot(
        jnp.broadcast_to(ids[...].astype(F32), (8, 128)).astype(BF16),
        (spot // 8 == elem).astype(F32).astype(BF16),
        preferred_element_type=F32,
    )
    for t in range(4):
        row = (lax.broadcasted_iota(jnp.int32, (8, 1024), 0) + 8 * t).astype(F32)
        onehot[pl.ds(8 * t, 8), :] = jnp.where(jnp.abs(wide - row) < 0.5, 1.0, 0.0)
    loads[10].wait()

    wait_halo(0, halo_recv)
    assemble_faces(0, local, image)

    coarse = []
    for m in range(3):
        total = get(image, m, rows_of(0)) * float(WEIGHTS[0])
        for p in range(1, 8):
            total += get(image, m, rows_of(p)) * float(WEIGHTS[p])
        total *= plane[0]
        acc = jnp.zeros((32, 256), F32)
        for b in range(4):
            line = jnp.sum(total[8 * b : 8 * b + 8], axis=0, keepdims=True)
            acc += onehot[:, pl.ds(256 * b, 256)] * line
        coarse.append(jnp.sum(acc, axis=1, keepdims=True))
    for j in range(PLANE):
        block = xxt[:, pl.ds(256 * j, 256)]
        for m in range(3):
            part_y[j, pl.ds(m, 1), :] = jnp.sum(block * coarse[m], axis=0, keepdims=True)

    def place_in_plane(peer):
        return lax.rem(peer[0], 4) * columns + peer[1]

    spread_out(
        0,
        in_plane,
        lambda peer: part_y.at[place_in_plane(peer)],
        lambda k: recv_y.at[k - 1],
    )
    apply_to_image(0)
    wait_bytes(recv_y, red_recv.at[0])
    total = part_y[here]
    for k in range(PLANE - 1):
        total += recv_y[k]
    sum_b[...] = total
    spread_out(1, in_ring, lambda peer: sum_b, lambda k: recv_b.at[k - 1])
    apply_to_image(1)
    wait_bytes(recv_b, red_recv.at[1])
    total = sum_b[...]
    for k in range(RING - 1):
        total += recv_b[k]
    all_y[here] = total
    spread_out(2, in_plane, lambda peer: all_y.at[here], lambda k: all_y.at[here])
    apply_to_image(2)
    wait_bytes(all_y.at[pl.ds(0, PLANE - 1)], red_recv.at[2])

    sums = [jnp.zeros((32, 256), F32) for _ in range(3)]
    for j in range(PLANE):
        block = xxt[:, pl.ds(256 * j, 256)]
        for m in range(3):
            sums[m] += block * all_y[j, pl.ds(m, 1), :]
    for m in range(3):
        column = jnp.sum(sums[m], axis=1, keepdims=True)
        for b in range(4):
            line = jnp.sum(onehot[:, pl.ds(256 * b, 256)] * column, axis=0, keepdims=True)
            cblock[m, pl.ds(8 * b, 8), :] = jnp.broadcast_to(line, (8, 256))

    def add_correction(m, p):
        rows = rows_of(p)
        total = cblock[0] * grads[m, 0, rows, :]
        total += cblock[1] * grads[m, 1, rows, :]
        total += cblock[2] * grads[m, 2, rows, :]
        put(local2, m, rows, get(local2, m, rows) + total * (plane[0] * float(WEIGHTS[p])))

    for m in range(3):
        add_correction(m, 0)
        add_correction(m, 7)
        send_x(1, local2, m)
    for m in range(3):
        for p in range(1, 7):
            add_correction(m, p)
    send_y(1, local2)
    for m in range(3):
        for p in range(8):
            probe[m, rows_of(p), :] = get(image, m, rows_of(p)) + cblock[m]
    probe_out = pltpu.make_async_copy(probe, probe_hbm, out_sem.at[0])
    probe_out.start()
    assemble_inside(local2, second)

    def weighed(value, weights):
        return jnp.sum(jnp.sum(value * weights, axis=0, keepdims=True), axis=1, keepdims=True)

    row32 = lax.broadcasted_iota(jnp.int32, (32, 1), 0) % 8
    inner = jnp.where((row32 == 0) | (row32 == 7), 0.0, plane[1])
    acc_in_sp, acc_in_pp, acc_pp = (jnp.zeros((32, 256), F32) for _ in range(3))
    for p in range(8):
        pp = jnp.zeros((32, 256), F32)
        for m in range(3):
            pr = probe[m, rows_of(p), :]
            pp += pr * pr
            if 0 < p < 7:
                acc_in_sp += get(second, m, rows_of(p)) * pr
        if 0 < p < 7:
            acc_in_pp += pp
        acc_pp += (0.5 if p in (0, 7) else 1.0) * pp
    in_sp, in_pp, pp = weighed(acc_in_sp, inner), weighed(acc_in_pp, inner), weighed(acc_pp, plane[1])
    own = jnp.where(in_pp > 0, in_sp / jnp.where(in_pp > 0, in_pp, 1.0), 0.0)

    wait_halo(1, halo_recv)
    assemble_faces(1, local2, second)
    second_out = [
        pltpu.make_async_copy(
            second.at[:, h], sec_hbm.at[:, :, pl.ds(128 * h, 128)], out_sem.at[1 + h]
        )
        for h in range(2)
    ]
    for out in second_out:
        out.start()
    acc_q, acc_rr = jnp.zeros((32, 256), F32), jnp.zeros((32, 256), F32)
    for p in range(8):
        q, rr = jnp.zeros((32, 256), F32), jnp.zeros((32, 256), F32)
        for m in range(3):
            pr = probe[m, rows_of(p), :]
            rest = get(second, m, rows_of(p)) - own * pr
            q += rest * pr
            rr += rest * rest
        scale = 0.5 if p in (0, 7) else 1.0
        acc_q += scale * q
        acc_rr += scale * rr
    q, rr = weighed(acc_q, plane[1]), weighed(acc_rr, plane[1])

    lane128 = lax.broadcasted_iota(jnp.int32, (1, 128), 1)

    def total_of(rows):
        return jnp.sum(rows, axis=0, keepdims=True)

    row_a[...] = jnp.where(
        lane128 < 32,
        own,
        jnp.where(lane128 < 64, q, jnp.where(lane128 < 96, pp, rr)),
    )
    spread_out(3, everyone, lambda peer: row_a, lambda k: recv_ra.at[pl.ds(k - 1, 1), :])
    recv_ra[pl.ds(255, 1), :] = row_a[...]
    wait_bytes(recv_ra.at[pl.ds(0, 255)], red_recv.at[3])
    own = recv_ra[...]
    q, pp, rr = (pltpu.roll(own, shift, 1) for shift in (96, 64, 32))
    weight_total = 343.0 * 128 * slabs * columns
    mean_sp, mean_pp = total_of(q + own * pp) / weight_total, total_of(pp) / weight_total
    coef = mean_sp / (mean_pp + epsilon)
    away = own - coef
    rest_mean = total_of(rr + 2.0 * away * q + away * away * pp) / weight_total
    rms = jnp.sqrt(jnp.maximum(rest_mean, 0.0) + epsilon)
    scal_ref[...] = jnp.concatenate([coef, rms, 1.0 / rms, jnp.zeros((5, 128), F32)], axis=0)

    wait_halo(0, halo_send)
    wait_halo(1, halo_send)
    wait_bytes(recv_y, red_send.at[0])
    wait_bytes(recv_b, red_send.at[1])
    wait_bytes(all_y.at[pl.ds(0, PLANE - 1)], red_send.at[2])
    wait_bytes(recv_ra.at[pl.ds(0, 255)], red_send.at[3])
    probe_out.wait()
    for out in second_out:
        out.wait()


def normalise(second_hbm, probe_hbm, scal_hbm, basis_hbm, hess, second, probe, scal, basis, sems):
    parts = [(m, pl.ds(128 * h, 128)) for m in range(3) for h in range(2)]
    scalars = pltpu.make_async_copy(scal_hbm, scal, sems.at[18])
    scalars.start()
    loads = []
    for i, (m, rows) in enumerate(parts):
        loads.append(
            [
                pltpu.make_async_copy(src.at[m, rows], dst.at[m, rows], sems.at[i + n])
                for src, dst, n in ((second_hbm, second, 0), (probe_hbm, probe, 6))
            ]
        )
        for load in loads[-1]:
            load.start()
    scalars.wait()
    coef, scale = scal[0:1, 0:1], scal[2:3, 0:1]
    hess[0] = scal[0, 0]
    hess[1] = scal[1, 0]
    stores = []
    for i, (m, rows) in enumerate(parts):
        for load in loads[i]:
            load.wait()
        for p in range(4):
            at = pl.ds(rows.start + 32 * p, 32)
            basis[m, at, :] = (second[m, at, :] - coef * probe[m, at, :]) * scale
        stores.append(
            pltpu.make_async_copy(basis.at[m, rows], basis_hbm.at[m, rows], sems.at[12 + i])
        )
        stores[-1].start()
    for store in stores:
        store.wait()


def shards(slabs, columns, state, direction, xxt_rows, coarse_ids):
    shape = state.shape
    left, right, plane, _ = constants()
    vmem = pltpu.VMEM
    field = (3, 256, 256)
    halved = (3, 2, 256, 128)

    def body(*refs):
        kernel(slabs, columns, *refs)

    anywhere = pl.BlockSpec(memory_space=pl.ANY)
    sec, probe, scal = pl.pallas_call(
        body,
        out_shape=(
            jax.ShapeDtypeStruct(field, F32),
            jax.ShapeDtypeStruct(field, F32),
            jax.ShapeDtypeStruct((8, 128), F32),
        ),
        in_specs=[pl.BlockSpec(memory_space=pltpu.HBM)] * 7,
        out_specs=(anywhere, anywhere, pl.BlockSpec(memory_space=vmem)),
        scratch_shapes=[
            vmem(field, F32),
            vmem(field, F32),
            vmem((32, 8192), F32),
            vmem((1, 128), jnp.int32),
            vmem((768, 512), BF16),
            vmem((512, 512), BF16),
            vmem((2, 32, 256), F32),
            vmem((2,) + field, BF16),
            vmem((2,) + field, BF16),
            vmem((3, 3, 256, 256), F32),
            vmem((3, 768, 256), F32),
            vmem((3, 256, 512), F32),
            vmem(halved, F32),
            vmem(halved, F32),
            vmem(halved, F32),
            vmem(halved, F32),
            vmem(field, F32),
            vmem((32, 1024), F32),
            vmem((3, 32, 256), F32),
            vmem((PLANE, 4, 256), F32),
            vmem((PLANE - 1, 4, 256), F32),
            vmem((4, 256), F32),
            vmem((RING - 1, 4, 256), F32),
            vmem((PLANE, 4, 256), F32),
            vmem((2, 3, 8, 256), F32),
            vmem((2, 3, 8, 256), F32),
            vmem((2, 4, 4, 256), F32),
            vmem((2, 3, 2, 32, 128), F32),
            vmem((2, 3, 2, 32, 128), F32),
            vmem((2, 3, 8, 256), F32),
            vmem((2, 3, 8, 256), F32),
            vmem((2, 4, 4, 256), F32),
            vmem((1, 128), F32),
            vmem((256, 128), F32),
            pltpu.SemaphoreType.DMA((11,)),
            pltpu.SemaphoreType.DMA((3,)),
            pltpu.SemaphoreType.DMA((2, 8)),
            pltpu.SemaphoreType.DMA((2, 8)),
            pltpu.SemaphoreType.DMA((4,)),
            pltpu.SemaphoreType.DMA((4,)),
        ],
        compiler_params=pltpu.CompilerParams(
            collective_id=0, has_side_effects=True, vmem_limit_bytes=VMEM_LIMIT
        ),
        name="jacobian_products",
    )(
        state.reshape(field),
        direction.reshape(field),
        xxt_rows,
        coarse_ids,
        jnp.asarray(left),
        jnp.asarray(right),
        jnp.asarray(plane),
    )
    next_basis, hessenberg = pl.pallas_call(
        normalise,
        out_shape=(jax.ShapeDtypeStruct(field, F32), jax.ShapeDtypeStruct((2,), F32)),
        in_specs=[pl.BlockSpec(memory_space=pltpu.HBM)] * 3,
        out_specs=(
            pl.BlockSpec(memory_space=pltpu.HBM),
            pl.BlockSpec(memory_space=pltpu.SMEM),
        ),
        scratch_shapes=[
            vmem(field, F32),
            vmem(field, F32),
            vmem((8, 128), F32),
            vmem(field, F32),
            pltpu.SemaphoreType.DMA((19,)),
        ],
        compiler_params=pltpu.CompilerParams(vmem_limit_bytes=VMEM_LIMIT),
        name="normalise",
    )(sec, probe, scal)
    return next_basis.reshape(shape), hessenberg


def solution(mesh):
    slabs, columns = mesh.shape["gx"], mesh.shape["yz"]

    def local_shards(*args):
        return shards(slabs, columns, *args)

    return jax.shard_map(
        local_shards,
        mesh=mesh,
        in_specs=(
            P(None, "gx", "yz", None),
            P(None, "gx", "yz", None),
            P(("gx", "yz"), None),
            P(("gx", "yz"), None),
        ),
        out_specs=(P(None, "gx", "yz", None), P()),
        check_vma=False,
    )
```

```python
import jax
import jax.numpy as jnp
import ml_dtypes
import numpy as np
from jax import lax
from jax.experimental import pallas as pl
from jax.experimental.pallas import tpu as pltpu
from jax.sharding import PartitionSpec as P

viscosity = 0.05
epsilon = 1e-06
MESH = pl.DeviceIdType.MESH
F32 = jnp.float32
BF16 = jnp.bfloat16
PLANE = 32
RING = 8
VMEM_LIMIT = 60 * 1024 * 1024


def tables():
    points = np.array(
        [
            -1.0,
            -0.8717401485096066,
            -0.5917001814331423,
            -0.2092992179024789,
            0.2092992179024789,
            0.5917001814331423,
            0.8717401485096066,
            1.0,
        ]
    )
    weights = np.array(
        [
            1.0 / 28.0,
            0.2107042271435061,
            0.3411226924835044,
            0.4124587946587038,
            0.4124587946587038,
            0.3411226924835044,
            0.2107042271435061,
            1.0 / 28.0,
        ]
    )
    differ = points[:, None] - points[None, :]
    positions = np.arange(8)
    differ[positions, positions] = 1.0
    barycentric = 1.0 / np.prod(differ, axis=1)
    derivative = barycentric[None, :] / barycentric[:, None] / differ
    derivative[positions, positions] = 0.0
    derivative[positions, positions] = -derivative.sum(axis=1)
    return derivative, weights


GROUPS = ((0, 64, (0, 7)), (192, 192, (1, 2, 3, 4, 5, 6)))
DIMS = {"z": 8, "x": 4, "y": 4, "c": 2}


def offsets(names):
    found = []
    for k in range(1, int(np.prod([DIMS[n] for n in names]))):
        place, hops, rest = {}, 0.0, k
        for n in reversed(names):
            place[n] = rest % DIMS[n]
            rest //= DIMS[n]
            near = min(place[n], DIMS[n] - place[n])
            hops += 0.25 * near if n == "c" else near
        found.append((-hops, k, place))
    return [(k, place) for _, k, place in sorted(found, key=lambda item: item[:2])]


def halves(matrix):
    high = matrix.astype(ml_dtypes.bfloat16)
    low = (matrix - high.astype(np.float64)).astype(ml_dtypes.bfloat16)
    return high, low


def constants():
    derivative, weights = tables()
    stiff = viscosity * (derivative.T * weights[None, :]) @ derivative / weights[:, None]
    eye = np.eye
    along_x = np.kron(derivative, eye(32))
    along_y = np.kron(eye(32), derivative)
    spread_xy = np.kron(stiff, eye(32)) + np.kron(eye(32), stiff)
    left = [
        op[32 * plane : 32 * plane + 32]
        for _, _, planes in GROUPS
        for op in (along_x, along_y, spread_xy)
        for plane in planes
    ]
    left = np.concatenate(left, axis=0)
    right = np.concatenate([np.kron(eye(16), derivative.T), np.kron(eye(16), stiff.T)], axis=1)
    left = np.concatenate(halves(left), axis=1)
    right = np.concatenate(halves(right), axis=0)
    return left, right


WEIGHTS = tables()[1]


def split(value):
    high = value.astype(BF16)
    return high, (value - high.astype(F32)).astype(BF16)


def kernel(
    slabs,
    columns,
    state_hbm,
    dir_hbm,
    xxt_hbm,
    ids_hbm,
    left_hbm,
    right_hbm,
    sec_hbm,
    probe_hbm,
    scal_ref,
    state,
    direc,
    xxt,
    ids,
    left,
    right,
    plane,
    highs,
    lows,
    grads,
    lhs_out,
    rhs_out,
    local,
    image,
    local2,
    second,
    probe,
    ysides,
    tsum,
    onehot,
    cblock,
    part_y,
    recv_y,
    sum_b,
    recv_b,
    all_y,
    send_yl,
    send_yh,
    send_c,
    recv_xl,
    recv_xh,
    recv_yl,
    recv_yh,
    recv_c,
    row_a,
    recv_ra,
    in_sem,
    out_sem,
    halo_send,
    halo_recv,
    red_send,
    red_recv,
):
    gx, yz = lax.axis_index("gx"), lax.axis_index("yz")
    gz, px = gx // 4, gx % 4
    here = px * columns + yz

    def peer_at(place):
        z = lax.rem(gz + place.get("z", 0), 8)
        x = lax.rem(px + place.get("x", 0), 4)
        y = lax.rem(yz // 2 + place.get("y", 0), 4)
        c = lax.rem(yz % 2 + place.get("c", 0), 2)
        return (z * 4 + x, y * 2 + c)

    in_plane, in_ring, everyone = offsets("xyc"), offsets("z"), offsets("zxyc")

    def beside(dx, dy):
        return (lax.rem(gx + dx + slabs, slabs), lax.rem(yz + dy + columns, columns))

    faces, inside_rows = pl.ds(0, 192), pl.ds(192, 576)
    pairs = [(left_hbm.at[faces], left.at[faces]), (right_hbm, right)]
    pairs += [(state_hbm.at[m], state.at[m]) for m in range(3)]
    pairs += [(dir_hbm.at[m], direc.at[m]) for m in range(3)]
    pairs += [(left_hbm.at[inside_rows], left.at[inside_rows])]
    pairs += [(ids_hbm, ids), (xxt_hbm, xxt)]
    loads = [pltpu.make_async_copy(src, dst, in_sem.at[i]) for i, (src, dst) in enumerate(pairs)]
    for load in loads[:-1]:
        load.start()

    barrier = pltpu.get_barrier_semaphore()
    greeted = [peer_at(place) for _, place in in_plane + in_ring]
    greeted += [beside(dx, dy) for dx in (-1, 1) for dy in (-1, 0, 1)]
    for peer in greeted:
        pl.semaphore_signal(barrier, inc=1, device_id=peer, device_id_type=MESH)

    lane = lax.broadcasted_iota(jnp.int32, (1, 256), 1)
    from_next = ((lane % 8 == 7) & (lane != 255)).astype(F32)
    from_last = ((lane % 8 == 0) & (lane != 0)).astype(F32)
    inside = ((lane != 0) & (lane != 255)).astype(F32)

    def by_place(place, values):
        place = place % 8
        place = jnp.minimum(place, 7 - place)
        result = jnp.full(place.shape, values[0], F32)
        for i in range(1, 4):
            result = jnp.where(place == i, float(values[i]), result)
        return result

    row32 = lax.broadcasted_iota(jnp.int32, (32, 1), 0)
    half = (0.5, 1.0, 1.0, 1.0)
    weights4 = [float(w) for w in WEIGHTS[:4]]
    plane[0] = by_place(row32, weights4) * by_place(lane, weights4)
    plane[1] = by_place(row32, half) * by_place(lane, half)
    wall_xl = jnp.where(gx == 0, 0.0, 1.0).astype(F32)
    wall_xh = jnp.where(gx == slabs - 1, 0.0, 1.0).astype(F32)
    wall_yl = jnp.where(yz == 0, 0.0, 1.0).astype(F32)
    wall_yh = jnp.where(yz == columns - 1, 0.0, 1.0).astype(F32)
    row8 = lax.broadcasted_iota(jnp.int32, (8, 1), 0)
    wall_x = jnp.where(row8 == 0, wall_xl, jnp.where(row8 == 7, wall_xh, 1.0))

    def fold_z(value):
        return (
            value * inside
            + pltpu.roll(value, 255, 1) * from_next
            + pltpu.roll(value, 1, 1) * from_last
        )

    def rows_of(p):
        return pl.ds(32 * p, 32)

    def get(ref, m, rows):
        return jnp.concatenate([ref[m, 0, rows, :], ref[m, 1, rows, :]], axis=1)

    def put(ref, m, rows, value):
        ref[m, 0, rows, :] = value[:, :128]
        ref[m, 1, rows, :] = value[:, 128:]

    def whole(ref, m, rows):
        return ref[m, rows, :]

    def split_into(value, which, m):
        high, low = split(value)
        highs[which, m] = high
        lows[which, m] = low

    def products_left(which, m, g, count):
        first, rows, _ = GROUPS[g]
        ops = left[pl.ds(first, rows * count), :]
        high, low = highs[which, m], lows[which, m]
        return jnp.dot(
            jnp.concatenate([ops, ops[:, :256]], axis=1),
            jnp.concatenate([high, high, low], axis=0),
            preferred_element_type=F32,
        )

    def products_right(which, m, g, cols):
        ops = right[:, pl.ds(0, cols)]
        ops = jnp.concatenate([ops, ops[:128]], axis=0)
        results = []
        for h in range(2):
            high, low = (
                jnp.concatenate(
                    [ref[which, m, rows_of(p), pl.ds(128 * h, 128)] for p in GROUPS[g][2]], axis=0
                )
                for ref in (highs, lows)
            )
            both = jnp.concatenate([high, high, low], axis=1)
            results.append(jnp.dot(both, ops, preferred_element_type=F32))
        return results

    def state_gradients(m, g):
        _, size, planes = GROUPS[g]
        by_left = products_left(0, m, g, 2)
        by_right = jnp.concatenate(products_right(0, m, g, 128), axis=1)
        for i, p in enumerate(planes):
            grads[m, 0, rows_of(p), :] = by_left[32 * i : 32 * i + 32]
            grads[m, 1, rows_of(p), :] = by_left[size + 32 * i : size + 32 * i + 32]
            grads[m, 2, rows_of(p), :] = by_right[32 * i : 32 * i + 32]

    def multiply(which, m, g):
        first, size, planes = GROUPS[g]
        lhs_out[m, pl.ds(first, 3 * size), :] = products_left(which, m, g, 3)
        for h, by_right in enumerate(products_right(which, m, g, 256)):
            for i, p in enumerate(planes):
                rhs_out[m, h, rows_of(p), :] = by_right[32 * i : 32 * i + 32]

    def along_z(m, rows, kind):
        part = pl.ds(128 * kind, 128)
        return jnp.concatenate([rhs_out[m, 0, rows, part], rhs_out[m, 1, rows, part]], axis=1)

    def combine(vector, take, m, g, target):
        first, size, planes = GROUPS[g]
        for i, p in enumerate(planes):
            rows = rows_of(p)
            at = [pl.ds(first + size * op + 32 * i, 32) for op in range(3)]
            total = lhs_out[m, at[2], :] + along_z(m, rows, 1)
            total += state[0, rows, :] * lhs_out[m, at[0], :]
            total += state[1, rows, :] * lhs_out[m, at[1], :]
            total += state[2, rows, :] * along_z(m, rows, 0)
            for k in range(3):
                total += take(vector, k, rows) * grads[m, k, rows, :]
            put(target, m, rows, total * (plane[0] * float(WEIGHTS[p])))

    def apply_to_image(m):
        split_into(get(image, m, pl.ds(0, 256)), 1, m)
        for g in range(2):
            multiply(1, m, g)
            combine(image, get, m, g, local2)

    def send(turn, index, src, dst, peer):
        pltpu.make_async_remote_copy(
            src_ref=src,
            dst_ref=dst,
            send_sem=halo_send.at[turn, index],
            recv_sem=halo_recv.at[turn, index],
            device_id=peer,
            device_id_type=MESH,
        ).start()

    def send_x(turn, source, m):
        send(turn, 0, source.at[m, :, pl.ds(224, 32), :], recv_xl.at[turn, m], beside(1, 0))
        send(turn, 1, source.at[m, :, pl.ds(0, 32), :], recv_xh.at[turn, m], beside(-1, 0))

    def send_corners(turn, source):
        for m in range(3):
            for i, row in enumerate((0, 31, 224, 255)):
                send_c[turn, i, pl.ds(m, 1), :] = get(source, m, pl.ds(row, 1))
        for i, (dx, dy) in enumerate(((-1, -1), (-1, 1), (1, -1), (1, 1))):
            send(turn, 4 + i, send_c.at[turn, i], recv_c.at[turn, i], beside(dx, dy))

    def send_y(turn, source, m):
        send_yl[turn, m] = get(source, m, pl.ds(0, 8, stride=32))
        send_yh[turn, m] = get(source, m, pl.ds(31, 8, stride=32))
        send(turn, 2, send_yh.at[turn, m], recv_yl.at[turn, m], beside(0, 1))
        send(turn, 3, send_yl.at[turn, m], recv_yh.at[turn, m], beside(0, -1))

    def halo_refs(turn):
        refs = [recv_xl.at[turn], recv_xh.at[turn], recv_yl.at[turn], recv_yh.at[turn]]
        return refs + [recv_c.at[turn, i] for i in range(4)]

    def wait_halo(turn, sems):
        for i, ref in enumerate(halo_refs(turn)):
            pltpu.make_async_copy(ref, ref, sems.at[turn, i]).wait()

    def fold_y(target, first, count, stride):
        for m in range(3):
            for b in range(3):
                one = pl.ds(first + 8 * b + 7, count, stride=stride)
                two = pl.ds(first + 8 * b + 8, count, stride=stride)
                both = get(target, m, one) + get(target, m, two)
                put(target, m, one, both)
                put(target, m, two, both)

    def assemble_planes(turn, source, target):
        for m in range(3):
            value = get(source, m, rows_of(0)) + get(recv_xl.at[turn], m, pl.ds(0, 32))
            put(target, m, rows_of(0), fold_z(value * wall_xl))
            value = get(source, m, rows_of(7)) + get(recv_xh.at[turn], m, pl.ds(0, 32))
            put(target, m, rows_of(7), fold_z(value * wall_xh))
            at_m = pl.ds(m, 1)
            low = recv_yl[turn, m]
            low += jnp.where(row8 == 0, recv_c[turn, 3, at_m, :], 0.0)
            low += jnp.where(row8 == 7, recv_c[turn, 1, at_m, :], 0.0)
            high = recv_yh[turn, m]
            high += jnp.where(row8 == 0, recv_c[turn, 2, at_m, :], 0.0)
            high += jnp.where(row8 == 7, recv_c[turn, 0, at_m, :], 0.0)
            ysides[0, m] = fold_z(low) * wall_x
            ysides[1, m] = fold_z(high) * wall_x

    def assemble_sides(target):
        first, last = pl.ds(0, 8, stride=32), pl.ds(31, 8, stride=32)
        for m in range(3):
            put(target, m, first, (get(target, m, first) + ysides[0, m]) * wall_yl)
            put(target, m, last, (get(target, m, last) + ysides[1, m]) * wall_yh)

    def spread_out(phase, places, src_of, dst_of):
        for k, place in places:
            peer = peer_at(place)
            pltpu.make_async_remote_copy(
                src_ref=src_of(peer),
                dst_ref=dst_of(k),
                send_sem=red_send.at[phase],
                recv_sem=red_recv.at[phase],
                device_id=peer,
                device_id_type=MESH,
            ).start()

    def wait_bytes(ref, sem):
        pltpu.make_async_copy(ref, ref, sem).wait()

    loads[0].wait()
    loads[1].wait()
    for m in range(3):
        loads[2 + m].wait()
        split_into(state[m], 0, m)
        state_gradients(m, 0)
    for m in range(3):
        loads[5 + m].wait()
        split_into(direc[m], 1, m)
    for m in range(3):
        multiply(1, m, 0)
        combine(direc, whole, m, 0, local)
        if m == 0:
            pl.semaphore_wait(barrier, len(greeted))
        send_x(0, local, m)
    send_corners(0, local)
    loads[10].start()
    loads[8].wait()
    for m in range(3):
        state_gradients(m, 1)
        multiply(1, m, 1)
        combine(direc, whole, m, 1, local)
        send_y(0, local, m)
    for m in range(3):
        total = jnp.zeros((32, 256), F32)
        for p in range(1, 7):
            value = fold_z(get(local, m, rows_of(p)))
            put(image, m, rows_of(p), value)
            total += float(WEIGHTS[p]) * value
        tsum[m] = total
    fold_y(image, 32, 6, 32)

    loads[9].wait()
    elem = lax.broadcasted_iota(jnp.int32, (128, 1024), 0)
    spot = lax.broadcasted_iota(jnp.int32, (128, 1024), 1)
    wide = jnp.dot(
        jnp.broadcast_to(ids[...].astype(F32), (8, 128)).astype(BF16),
        (spot // 8 == elem).astype(F32).astype(BF16),
        preferred_element_type=F32,
    )
    for t in range(4):
        row = (lax.broadcasted_iota(jnp.int32, (8, 1024), 0) + 8 * t).astype(F32)
        onehot[pl.ds(8 * t, 8), :] = jnp.where(jnp.abs(wide - row) < 0.5, 1.0, 0.0)
    loads[10].wait()

    wait_halo(0, halo_recv)
    assemble_planes(0, local, image)

    weight8 = by_place(row8, weights4)
    y_next = ((row32 % 8 == 7) & (row32 != 31)).astype(F32)
    y_last = ((row32 % 8 == 0) & (row32 != 0)).astype(F32)
    wall_y = jnp.where(row32 == 0, wall_yl, jnp.where(row32 == 31, wall_yh, 1.0))
    coarse = []
    for m in range(3):
        total = tsum[m] + float(WEIGHTS[0]) * (get(image, m, rows_of(0)) + get(image, m, rows_of(7)))
        low, high = (
            jnp.sum(ysides[i, m] * weight8, axis=0, keepdims=True) for i in range(2)
        )
        total += jnp.where(row32 == 0, low, 0.0) + jnp.where(row32 == 31, high, 0.0)
        folded = total + pltpu.roll(total, 31, 0) * y_next + pltpu.roll(total, 1, 0) * y_last
        folded *= plane[0] * wall_y
        acc = jnp.zeros((32, 256), F32)
        for b in range(4):
            line = jnp.sum(folded[8 * b : 8 * b + 8], axis=0, keepdims=True)
            acc += onehot[:, pl.ds(256 * b, 256)] * line
        coarse.append(jnp.sum(acc, axis=1, keepdims=True))

    def form_part(slot, peer):
        chunk = lax.rem(peer[0], 4) * columns + peer[1]
        block = xxt[:, pl.ds(pl.multiple_of(chunk * 256, 256), 256)]
        for m in range(3):
            part_y[slot, pl.ds(m, 1), :] = jnp.sum(block * coarse[m], axis=0, keepdims=True)

    for k, place in in_plane:
        form_part(k, peer_at(place))
        spread_out(0, [(k, place)], lambda peer: part_y.at[k], lambda k: recv_y.at[k - 1])
    form_part(0, (gx, yz))
    assemble_sides(image)
    fold_y(image, 0, 2, 224)
    apply_to_image(0)
    wait_bytes(recv_y, red_recv.at[0])
    total = part_y[0]
    for k in range(PLANE - 1):
        total += recv_y[k]
    sum_b[...] = total
    spread_out(1, in_ring, lambda peer: sum_b, lambda k: recv_b.at[k - 1])
    apply_to_image(1)
    wait_bytes(recv_b, red_recv.at[1])
    total = sum_b[...]
    for k in range(RING - 1):
        total += recv_b[k]
    all_y[here] = total
    spread_out(2, in_plane, lambda peer: all_y.at[here], lambda k: all_y.at[here])
    apply_to_image(2)
    wait_bytes(all_y.at[pl.ds(0, PLANE - 1)], red_recv.at[2])

    sums = [jnp.zeros((32, 256), F32) for _ in range(3)]
    for j in range(PLANE):
        block = xxt[:, pl.ds(256 * j, 256)]
        for m in range(3):
            sums[m] += block * all_y[j, pl.ds(m, 1), :]
    for m in range(3):
        column = jnp.sum(sums[m], axis=1, keepdims=True)
        for b in range(4):
            line = jnp.sum(onehot[:, pl.ds(256 * b, 256)] * column, axis=0, keepdims=True)
            cblock[m, pl.ds(8 * b, 8), :] = jnp.broadcast_to(line, (8, 256))

    def add_correction(m, p):
        rows = rows_of(p)
        total = cblock[0] * grads[m, 0, rows, :]
        total += cblock[1] * grads[m, 1, rows, :]
        total += cblock[2] * grads[m, 2, rows, :]
        put(local2, m, rows, get(local2, m, rows) + total * (plane[0] * float(WEIGHTS[p])))

    for m in range(3):
        add_correction(m, 0)
        add_correction(m, 7)
        send_x(1, local2, m)
    send_corners(1, local2)
    for m in range(3):
        for p in range(1, 7):
            add_correction(m, p)
        send_y(1, local2, m)
    for m in range(3):
        for p in range(8):
            put(probe, m, rows_of(p), get(image, m, rows_of(p)) + cblock[m])

    def copies_out(source, target, n):
        copies = [
            pltpu.make_async_copy(
                source.at[:, h], target.at[:, :, pl.ds(128 * h, 128)], out_sem.at[n + h]
            )
            for h in range(2)
        ]
        for copy in copies:
            copy.start()
        return copies

    outs = copies_out(probe, probe_hbm, 0)
    for m in range(3):
        for p in range(1, 7):
            put(second, m, rows_of(p), fold_z(get(local2, m, rows_of(p))))

    def weighed(value, weights):
        return jnp.sum(jnp.sum(value * weights, axis=0, keepdims=True), axis=1, keepdims=True)

    inner = jnp.where((row32 % 8 == 0) | (row32 % 8 == 7), 0.0, plane[1])
    acc_in_sp, acc_in_pp, acc_pp = (jnp.zeros((32, 256), F32) for _ in range(3))
    for p in range(8):
        pp = jnp.zeros((32, 256), F32)
        for m in range(3):
            pr = get(probe, m, rows_of(p))
            pp += pr * pr
            if 0 < p < 7:
                acc_in_sp += get(second, m, rows_of(p)) * pr
        if 0 < p < 7:
            acc_in_pp += pp
        acc_pp += (0.5 if p in (0, 7) else 1.0) * pp
    in_sp, in_pp, pp = (
        weighed(acc_in_sp, inner),
        weighed(acc_in_pp, inner),
        weighed(acc_pp, plane[1]),
    )
    own = jnp.where(in_pp > 0, in_sp / jnp.where(in_pp > 0, in_pp, 1.0), 0.0)
    fold_y(second, 32, 6, 32)

    def residual_sums(places):
        q, rr = 0.0, 0.0
        for rows in places:
            for m in range(3):
                pr = get(probe, m, rows)
                rest = get(second, m, rows) - own * pr
                q += rest * pr
                rr += rest * rest
        return q, rr

    not_sides = jnp.where((row32 == 0) | (row32 == 31), 0.0, plane[1])
    sums_in = [v * not_sides for v in residual_sums([rows_of(p) for p in range(1, 7)])]

    wait_halo(1, halo_recv)
    assemble_planes(1, local2, second)
    assemble_sides(second)
    fold_y(second, 0, 2, 224)
    outs += copies_out(second, sec_hbm, 2)
    sums_faces = residual_sums([rows_of(0), rows_of(7)])
    sums_sides = residual_sums([pl.ds(32, 6, stride=32), pl.ds(63, 6, stride=32)])
    q, rr = (
        jnp.sum(
            jnp.sum(one + two * (0.5 * plane[1]), axis=0, keepdims=True)
            + jnp.sum(three, axis=0, keepdims=True) * plane[1, 0:1, :],
            axis=1,
            keepdims=True,
        )
        for one, two, three in zip(sums_in, sums_faces, sums_sides)
    )

    lane128 = lax.broadcasted_iota(jnp.int32, (1, 128), 1)

    def total_of(rows):
        return jnp.sum(rows, axis=0, keepdims=True)

    row_a[...] = jnp.where(
        lane128 < 32,
        own,
        jnp.where(lane128 < 64, q, jnp.where(lane128 < 96, pp, rr)),
    )
    spread_out(3, everyone, lambda peer: row_a, lambda k: recv_ra.at[pl.ds(k - 1, 1), :])
    recv_ra[pl.ds(255, 1), :] = row_a[...]
    wait_bytes(recv_ra.at[pl.ds(0, 255)], red_recv.at[3])
    own = recv_ra[...]
    q, pp, rr = (pltpu.roll(own, shift, 1) for shift in (96, 64, 32))
    weight_total = 343.0 * 128 * slabs * columns
    mean_sp, mean_pp = total_of(q + own * pp) / weight_total, total_of(pp) / weight_total
    coef = mean_sp / (mean_pp + epsilon)
    away = own - coef
    rest_mean = total_of(rr + 2.0 * away * q + away * away * pp) / weight_total
    rms = jnp.sqrt(jnp.maximum(rest_mean, 0.0) + epsilon)
    scal_ref[...] = jnp.concatenate([coef, rms, 1.0 / rms, jnp.zeros((5, 128), F32)], axis=0)

    wait_halo(0, halo_send)
    wait_halo(1, halo_send)
    wait_bytes(recv_y, red_send.at[0])
    wait_bytes(recv_b, red_send.at[1])
    wait_bytes(all_y.at[pl.ds(0, PLANE - 1)], red_send.at[2])
    wait_bytes(recv_ra.at[pl.ds(0, 255)], red_send.at[3])
    for out in outs:
        out.wait()


def normalise(second_hbm, probe_hbm, scal_hbm, basis_hbm, hess, second, probe, scal, basis, sems):
    parts = [(m, pl.ds(128 * h, 128)) for m in range(3) for h in range(2)]
    scalars = pltpu.make_async_copy(scal_hbm, scal, sems.at[18])
    scalars.start()
    loads = []
    for i, (m, rows) in enumerate(parts):
        loads.append(
            [
                pltpu.make_async_copy(src.at[m, rows], dst.at[m, rows], sems.at[i + n])
                for src, dst, n in ((second_hbm, second, 0), (probe_hbm, probe, 6))
            ]
        )
        for load in loads[-1]:
            load.start()
    scalars.wait()
    coef, scale = scal[0:1, 0:1], scal[2:3, 0:1]
    hess[0] = scal[0, 0]
    hess[1] = scal[1, 0]
    stores = []
    for i, (m, rows) in enumerate(parts):
        for load in loads[i]:
            load.wait()
        for p in range(4):
            at = pl.ds(rows.start + 32 * p, 32)
            basis[m, at, :] = (second[m, at, :] - coef * probe[m, at, :]) * scale
        stores.append(
            pltpu.make_async_copy(basis.at[m, rows], basis_hbm.at[m, rows], sems.at[12 + i])
        )
        stores[-1].start()
    for store in stores:
        store.wait()


def shards(slabs, columns, state, direction, xxt_rows, coarse_ids):
    shape = state.shape
    left, right = constants()
    vmem = pltpu.VMEM
    field = (3, 256, 256)
    halved = (3, 2, 256, 128)

    def body(*refs):
        kernel(slabs, columns, *refs)

    anywhere = pl.BlockSpec(memory_space=pl.ANY)
    sec, probe, scal = pl.pallas_call(
        body,
        out_shape=(
            jax.ShapeDtypeStruct(field, F32),
            jax.ShapeDtypeStruct(field, F32),
            jax.ShapeDtypeStruct((8, 128), F32),
        ),
        in_specs=[pl.BlockSpec(memory_space=pltpu.HBM)] * 6,
        out_specs=(anywhere, anywhere, pl.BlockSpec(memory_space=vmem)),
        scratch_shapes=[
            vmem(field, F32),
            vmem(field, F32),
            vmem((32, 8192), F32),
            vmem((1, 128), jnp.int32),
            vmem((768, 512), BF16),
            vmem((256, 256), BF16),
            vmem((2, 32, 256), F32),
            vmem((2,) + field, BF16),
            vmem((2,) + field, BF16),
            vmem((3, 3, 256, 256), F32),
            vmem((3, 768, 256), F32),
            vmem((3, 2, 256, 256), F32),
            vmem(halved, F32),
            vmem(halved, F32),
            vmem(halved, F32),
            vmem(halved, F32),
            vmem(halved, F32),
            vmem((2, 3, 8, 256), F32),
            vmem((3, 32, 256), F32),
            vmem((32, 1024), F32),
            vmem((3, 32, 256), F32),
            vmem((PLANE, 4, 256), F32),
            vmem((PLANE - 1, 4, 256), F32),
            vmem((4, 256), F32),
            vmem((RING - 1, 4, 256), F32),
            vmem((PLANE, 4, 256), F32),
            vmem((2, 3, 8, 256), F32),
            vmem((2, 3, 8, 256), F32),
            vmem((2, 4, 4, 256), F32),
            vmem((2, 3, 2, 32, 128), F32),
            vmem((2, 3, 2, 32, 128), F32),
            vmem((2, 3, 8, 256), F32),
            vmem((2, 3, 8, 256), F32),
            vmem((2, 4, 4, 256), F32),
            vmem((1, 128), F32),
            vmem((256, 128), F32),
            pltpu.SemaphoreType.DMA((11,)),
            pltpu.SemaphoreType.DMA((4,)),
            pltpu.SemaphoreType.DMA((2, 8)),
            pltpu.SemaphoreType.DMA((2, 8)),
            pltpu.SemaphoreType.DMA((4,)),
            pltpu.SemaphoreType.DMA((4,)),
        ],
        compiler_params=pltpu.CompilerParams(
            collective_id=0, has_side_effects=True, vmem_limit_bytes=VMEM_LIMIT
        ),
        name="jacobian_products",
    )(
        state.reshape(field),
        direction.reshape(field),
        xxt_rows,
        coarse_ids,
        jnp.asarray(left),
        jnp.asarray(right),
    )
    next_basis, hessenberg = pl.pallas_call(
        normalise,
        out_shape=(jax.ShapeDtypeStruct(field, F32), jax.ShapeDtypeStruct((2,), F32)),
        in_specs=[pl.BlockSpec(memory_space=pltpu.HBM)] * 3,
        out_specs=(
            pl.BlockSpec(memory_space=pltpu.HBM),
            pl.BlockSpec(memory_space=pltpu.SMEM),
        ),
        scratch_shapes=[
            vmem(field, F32),
            vmem(field, F32),
            vmem((8, 128), F32),
            vmem(field, F32),
            pltpu.SemaphoreType.DMA((19,)),
        ],
        compiler_params=pltpu.CompilerParams(vmem_limit_bytes=VMEM_LIMIT),
        name="normalise",
    )(sec, probe, scal)
    return next_basis.reshape(shape), hessenberg


def solution(mesh):
    slabs, columns = mesh.shape["gx"], mesh.shape["yz"]

    def local_shards(*args):
        return shards(slabs, columns, *args)

    return jax.shard_map(
        local_shards,
        mesh=mesh,
        in_specs=(
            P(None, "gx", "yz", None),
            P(None, "gx", "yz", None),
            P(("gx", "yz"), None),
            P(("gx", "yz"), None),
        ),
        out_specs=(P(None, "gx", "yz", None), P()),
        check_vma=False,
    )
```

```python
import jax
import jax.numpy as jnp
import ml_dtypes
import numpy as np
from jax import lax
from jax.experimental import pallas as pl
from jax.experimental.pallas import tpu as pltpu
from jax.sharding import PartitionSpec as P

viscosity = 0.05
epsilon = 1e-06
MESH = pl.DeviceIdType.MESH
F32 = jnp.float32
BF16 = jnp.bfloat16
PLANE = 32
RING = 8
VMEM_LIMIT = 52 * 1024 * 1024


def tables():
    points = np.array(
        [
            -1.0,
            -0.8717401485096066,
            -0.5917001814331423,
            -0.2092992179024789,
            0.2092992179024789,
            0.5917001814331423,
            0.8717401485096066,
            1.0,
        ]
    )
    weights = np.array(
        [
            1.0 / 28.0,
            0.2107042271435061,
            0.3411226924835044,
            0.4124587946587038,
            0.4124587946587038,
            0.3411226924835044,
            0.2107042271435061,
            1.0 / 28.0,
        ]
    )
    differ = points[:, None] - points[None, :]
    positions = np.arange(8)
    differ[positions, positions] = 1.0
    barycentric = 1.0 / np.prod(differ, axis=1)
    derivative = barycentric[None, :] / barycentric[:, None] / differ
    derivative[positions, positions] = 0.0
    derivative[positions, positions] = -derivative.sum(axis=1)
    return derivative, weights


GROUPS = ((0, 64, (0, 7)), (192, 192, (1, 2, 3, 4, 5, 6)))
DIMS = {"z": 8, "x": 4, "y": 4, "c": 2}


def offsets(names):
    found = []
    for k in range(1, int(np.prod([DIMS[n] for n in names]))):
        place, hops, rest = {}, 0.0, k
        for n in reversed(names):
            place[n] = rest % DIMS[n]
            rest //= DIMS[n]
            near = min(place[n], DIMS[n] - place[n])
            hops += 0.25 * near if n == "c" else near
        found.append((-hops, k, place))
    return [(k, place) for _, k, place in sorted(found, key=lambda item: item[:2])]


def halves(matrix):
    high = matrix.astype(ml_dtypes.bfloat16)
    low = (matrix - high.astype(np.float64)).astype(ml_dtypes.bfloat16)
    return high, low


def constants():
    derivative, weights = tables()
    stiff = viscosity * (derivative.T * weights[None, :]) @ derivative / weights[:, None]
    eye = np.eye
    along_x = np.kron(derivative, eye(32))
    along_y = np.kron(eye(32), derivative)
    spread_xy = np.kron(stiff, eye(32)) + np.kron(eye(32), stiff)
    left = [
        op[32 * plane : 32 * plane + 32]
        for _, _, planes in GROUPS
        for op in (along_x, along_y, spread_xy)
        for plane in planes
    ]
    left = np.concatenate(left, axis=0)
    right = np.concatenate([np.kron(eye(16), derivative.T), np.kron(eye(16), stiff.T)], axis=1)
    return np.concatenate(
        [
            np.concatenate(halves(left[:192]), axis=1),
            np.concatenate(halves(right), axis=1),
            np.concatenate(halves(left[192:]), axis=1),
        ],
        axis=0,
    )


WEIGHTS = tables()[1]


def split(value):
    high = value.astype(BF16)
    return high, (value - high.astype(F32)).astype(BF16)


def kernel(
    slabs,
    columns,
    state_hbm,
    dir_hbm,
    xxt_hbm,
    ids_hbm,
    ops_hbm,
    sec_hbm,
    probe_hbm,
    scal_ref,
    state,
    direc,
    xxt,
    ids,
    ops_all,
    plane,
    highs,
    lows,
    grads,
    lhs_out,
    rhs_out,
    local,
    image,
    local2,
    second,
    probe,
    ysides,
    tsum,
    onehot,
    cblock,
    part_y,
    recv_y,
    sum_b,
    recv_b,
    all_y,
    send_yl,
    send_yh,
    send_c,
    recv_xl,
    recv_xh,
    recv_yl,
    recv_yh,
    recv_c,
    row_a,
    recv_ra,
    in_sem,
    out_sem,
    halo_send,
    halo_recv,
    red_send,
    red_recv,
):
    gx, yz = lax.axis_index("gx"), lax.axis_index("yz")
    gz, px = gx // 4, gx % 4
    here = px * columns + yz

    def peer_at(place):
        z = lax.rem(gz + place.get("z", 0), 8)
        x = lax.rem(px + place.get("x", 0), 4)
        y = lax.rem(yz // 2 + place.get("y", 0), 4)
        c = lax.rem(yz % 2 + place.get("c", 0), 2)
        return (z * 4 + x, y * 2 + c)

    in_plane, in_ring, everyone = offsets("xyc"), offsets("z"), offsets("zxyc")

    def beside(dx, dy):
        return (lax.rem(gx + dx + slabs, slabs), lax.rem(yz + dy + columns, columns))

    first, others = pl.ds(0, 320), pl.ds(320, 576)
    pairs = [(ops_hbm.at[first], ops_all.at[first])]
    pairs += [(state_hbm.at[m], state.at[m]) for m in range(3)]
    pairs += [(dir_hbm.at[m], direc.at[m]) for m in range(3)]
    pairs += [(ops_hbm.at[others], ops_all.at[others])]
    pairs += [(ids_hbm, ids), (xxt_hbm, xxt)]
    loads = [pltpu.make_async_copy(src, dst, in_sem.at[i]) for i, (src, dst) in enumerate(pairs)]
    for load in loads[:-1]:
        load.start()

    barrier = pltpu.get_barrier_semaphore()
    greeted = [peer_at(place) for _, place in in_plane + in_ring]
    greeted += [beside(dx, dy) for dx in (-1, 1) for dy in (-1, 0, 1)]
    for peer in greeted:
        pl.semaphore_signal(barrier, inc=1, device_id=peer, device_id_type=MESH)

    lane = lax.broadcasted_iota(jnp.int32, (1, 256), 1)
    from_next = ((lane % 8 == 7) & (lane != 255)).astype(F32)
    from_last = ((lane % 8 == 0) & (lane != 0)).astype(F32)
    inside = ((lane != 0) & (lane != 255)).astype(F32)

    def by_place(place, values):
        place = place % 8
        place = jnp.minimum(place, 7 - place)
        result = jnp.full(place.shape, values[0], F32)
        for i in range(1, 4):
            result = jnp.where(place == i, float(values[i]), result)
        return result

    row32 = lax.broadcasted_iota(jnp.int32, (32, 1), 0)
    half = (0.5, 1.0, 1.0, 1.0)
    weights4 = [float(w) for w in WEIGHTS[:4]]
    plane[0] = by_place(row32, weights4) * by_place(lane, weights4)
    plane[1] = by_place(row32, half) * by_place(lane, half)
    wall_xl = jnp.where(gx == 0, 0.0, 1.0).astype(F32)
    wall_xh = jnp.where(gx == slabs - 1, 0.0, 1.0).astype(F32)
    wall_yl = jnp.where(yz == 0, 0.0, 1.0).astype(F32)
    wall_yh = jnp.where(yz == columns - 1, 0.0, 1.0).astype(F32)
    row8 = lax.broadcasted_iota(jnp.int32, (8, 1), 0)
    wall_x = jnp.where(row8 == 0, wall_xl, jnp.where(row8 == 7, wall_xh, 1.0))

    def fold_z(value):
        return (
            value * inside
            + pltpu.roll(value, 255, 1) * from_next
            + pltpu.roll(value, 1, 1) * from_last
        )

    def rows_of(p):
        return pl.ds(32 * p, 32)

    def get(ref, m, rows):
        return jnp.concatenate([ref[m, 0, rows, :], ref[m, 1, rows, :]], axis=1)

    def put(ref, m, rows, value):
        ref[m, 0, rows, :] = value[:, :128]
        ref[m, 1, rows, :] = value[:, 128:]

    def whole(ref, m, rows):
        return ref[m, rows, :]

    def split_into(value, which, m):
        high, low = split(value)
        highs[which, m] = high
        lows[which, m] = low

    def products_left(which, m, g, count):
        first, rows, _ = GROUPS[g]
        ops = ops_all[pl.ds(first + 128 * g, rows * count), :]
        high, low = highs[which, m], lows[which, m]
        return jnp.dot(
            jnp.concatenate([ops, ops[:, :256]], axis=1),
            jnp.concatenate([high, high, low], axis=0),
            preferred_element_type=F32,
        )

    def products_right(which, m, g, cols):
        at = pl.ds(192, 128)
        high, low = (ops_all[at, pl.ds(start, cols)] for start in (0, 256))
        ops = jnp.concatenate([high, low, high], axis=0)
        results = []
        for h in range(2):
            high, low = (
                jnp.concatenate(
                    [ref[which, m, rows_of(p), pl.ds(128 * h, 128)] for p in GROUPS[g][2]], axis=0
                )
                for ref in (highs, lows)
            )
            both = jnp.concatenate([high, high, low], axis=1)
            results.append(jnp.dot(both, ops, preferred_element_type=F32))
        return results

    def state_gradients(m, g):
        _, size, planes = GROUPS[g]
        by_left = products_left(0, m, g, 2)
        by_right = jnp.concatenate(products_right(0, m, g, 128), axis=1)
        for i, p in enumerate(planes):
            grads[m, 0, rows_of(p), :] = by_left[32 * i : 32 * i + 32]
            grads[m, 1, rows_of(p), :] = by_left[size + 32 * i : size + 32 * i + 32]
            grads[m, 2, rows_of(p), :] = by_right[32 * i : 32 * i + 32]

    def multiply(which, m, g):
        first, size, planes = GROUPS[g]
        lhs_out[m, pl.ds(first, 3 * size), :] = products_left(which, m, g, 3)
        for h, by_right in enumerate(products_right(which, m, g, 256)):
            for i, p in enumerate(planes):
                rhs_out[m, h, rows_of(p), :] = by_right[32 * i : 32 * i + 32]

    def along_z(m, rows, kind):
        part = pl.ds(128 * kind, 128)
        return jnp.concatenate([rhs_out[m, 0, rows, part], rhs_out[m, 1, rows, part]], axis=1)

    def combine(vector, take, m, g, target):
        first, size, planes = GROUPS[g]
        for i, p in enumerate(planes):
            rows = rows_of(p)
            at = [pl.ds(first + size * op + 32 * i, 32) for op in range(3)]
            total = lhs_out[m, at[2], :] + along_z(m, rows, 1)
            total += state[0, rows, :] * lhs_out[m, at[0], :]
            total += state[1, rows, :] * lhs_out[m, at[1], :]
            total += state[2, rows, :] * along_z(m, rows, 0)
            for k in range(3):
                total += take(vector, k, rows) * grads[m, k, rows, :]
            put(target, m, rows, total * (plane[0] * float(WEIGHTS[p])))

    def apply_to_image(m):
        split_into(get(image, m, pl.ds(0, 256)), 1, m)
        for g in range(2):
            multiply(1, m, g)
            combine(image, get, m, g, local2)

    def send(turn, index, src, dst, peer):
        pltpu.make_async_remote_copy(
            src_ref=src,
            dst_ref=dst,
            send_sem=halo_send.at[turn, index],
            recv_sem=halo_recv.at[turn, index],
            device_id=peer,
            device_id_type=MESH,
        ).start()

    def send_x(turn, source, m):
        send(turn, 0, source.at[m, :, pl.ds(224, 32), :], recv_xl.at[turn, m], beside(1, 0))
        send(turn, 1, source.at[m, :, pl.ds(0, 32), :], recv_xh.at[turn, m], beside(-1, 0))

    def send_corners(turn, source):
        for m in range(3):
            for i, row in enumerate((0, 31, 224, 255)):
                send_c[turn, i, pl.ds(m, 1), :] = get(source, m, pl.ds(row, 1))
        for i, (dx, dy) in enumerate(((-1, -1), (-1, 1), (1, -1), (1, 1))):
            send(turn, 4 + i, send_c.at[turn, i], recv_c.at[turn, i], beside(dx, dy))

    def send_y(turn, source, m):
        send_yl[turn, m] = get(source, m, pl.ds(0, 8, stride=32))
        send_yh[turn, m] = get(source, m, pl.ds(31, 8, stride=32))
        send(turn, 2, send_yh.at[turn, m], recv_yl.at[turn, m], beside(0, 1))
        send(turn, 3, send_yl.at[turn, m], recv_yh.at[turn, m], beside(0, -1))

    def halo_refs(turn):
        refs = [recv_xl.at[turn], recv_xh.at[turn], recv_yl.at[turn], recv_yh.at[turn]]
        return refs + [recv_c.at[turn, i] for i in range(4)]

    def wait_halo(turn, sems):
        for i, ref in enumerate(halo_refs(turn)):
            pltpu.make_async_copy(ref, ref, sems.at[turn, i]).wait()

    def fold_y(target, first, count, stride):
        for m in range(3):
            for b in range(3):
                one = pl.ds(first + 8 * b + 7, count, stride=stride)
                two = pl.ds(first + 8 * b + 8, count, stride=stride)
                both = get(target, m, one) + get(target, m, two)
                put(target, m, one, both)
                put(target, m, two, both)

    def assemble_planes(turn, source, target):
        for m in range(3):
            value = get(source, m, rows_of(0)) + get(recv_xl.at[turn], m, pl.ds(0, 32))
            put(target, m, rows_of(0), fold_z(value * wall_xl))
            value = get(source, m, rows_of(7)) + get(recv_xh.at[turn], m, pl.ds(0, 32))
            put(target, m, rows_of(7), fold_z(value * wall_xh))
            at_m = pl.ds(m, 1)
            low = recv_yl[turn, m]
            low += jnp.where(row8 == 0, recv_c[turn, 3, at_m, :], 0.0)
            low += jnp.where(row8 == 7, recv_c[turn, 1, at_m, :], 0.0)
            high = recv_yh[turn, m]
            high += jnp.where(row8 == 0, recv_c[turn, 2, at_m, :], 0.0)
            high += jnp.where(row8 == 7, recv_c[turn, 0, at_m, :], 0.0)
            ysides[0, m] = fold_z(low) * wall_x
            ysides[1, m] = fold_z(high) * wall_x

    def assemble_sides(target):
        first, last = pl.ds(0, 8, stride=32), pl.ds(31, 8, stride=32)
        for m in range(3):
            put(target, m, first, (get(target, m, first) + ysides[0, m]) * wall_yl)
            put(target, m, last, (get(target, m, last) + ysides[1, m]) * wall_yh)

    def spread_out(phase, places, src_of, dst_of):
        for k, place in places:
            peer = peer_at(place)
            pltpu.make_async_remote_copy(
                src_ref=src_of(peer),
                dst_ref=dst_of(k),
                send_sem=red_send.at[phase],
                recv_sem=red_recv.at[phase],
                device_id=peer,
                device_id_type=MESH,
            ).start()

    def wait_bytes(ref, sem):
        pltpu.make_async_copy(ref, ref, sem).wait()

    loads[0].wait()
    for m in range(3):
        loads[1 + m].wait()
        split_into(state[m], 0, m)
        state_gradients(m, 0)
    for m in range(3):
        loads[4 + m].wait()
        split_into(direc[m], 1, m)
    for m in range(3):
        multiply(1, m, 0)
        combine(direc, whole, m, 0, local)
        if m == 0:
            pl.semaphore_wait(barrier, len(greeted))
        send_x(0, local, m)
    send_corners(0, local)
    loads[9].start()
    loads[7].wait()
    for m in range(3):
        state_gradients(m, 1)
        multiply(1, m, 1)
        combine(direc, whole, m, 1, local)
        send_y(0, local, m)
    for m in range(3):
        total = jnp.zeros((32, 256), F32)
        for p in range(1, 7):
            value = fold_z(get(local, m, rows_of(p)))
            put(image, m, rows_of(p), value)
            total += float(WEIGHTS[p]) * value
        tsum[m] = total
    fold_y(image, 32, 6, 32)

    loads[8].wait()
    elem = lax.broadcasted_iota(jnp.int32, (128, 1024), 0)
    spot = lax.broadcasted_iota(jnp.int32, (128, 1024), 1)
    wide = jnp.dot(
        jnp.broadcast_to(ids[...].astype(F32), (8, 128)).astype(BF16),
        (spot // 8 == elem).astype(F32).astype(BF16),
        preferred_element_type=F32,
    )
    for t in range(4):
        row = (lax.broadcasted_iota(jnp.int32, (8, 1024), 0) + 8 * t).astype(F32)
        onehot[pl.ds(8 * t, 8), :] = jnp.where(jnp.abs(wide - row) < 0.5, 1.0, 0.0)
    loads[9].wait()

    wait_halo(0, halo_recv)
    assemble_planes(0, local, image)

    weight8 = by_place(row8, weights4)
    y_next = ((row32 % 8 == 7) & (row32 != 31)).astype(F32)
    y_last = ((row32 % 8 == 0) & (row32 != 0)).astype(F32)
    wall_y = jnp.where(row32 == 0, wall_yl, jnp.where(row32 == 31, wall_yh, 1.0))
    coarse = []
    for m in range(3):
        total = tsum[m] + float(WEIGHTS[0]) * (get(image, m, rows_of(0)) + get(image, m, rows_of(7)))
        low, high = (
            jnp.sum(ysides[i, m] * weight8, axis=0, keepdims=True) for i in range(2)
        )
        total += jnp.where(row32 == 0, low, 0.0) + jnp.where(row32 == 31, high, 0.0)
        folded = total + pltpu.roll(total, 31, 0) * y_next + pltpu.roll(total, 1, 0) * y_last
        folded *= plane[0] * wall_y
        acc = jnp.zeros((32, 256), F32)
        for b in range(4):
            line = jnp.sum(folded[8 * b : 8 * b + 8], axis=0, keepdims=True)
            acc += onehot[:, pl.ds(256 * b, 256)] * line
        coarse.append(jnp.sum(acc, axis=1, keepdims=True))

    def form_part(slot, peer):
        chunk = lax.rem(peer[0], 4) * columns + peer[1]
        block = xxt[:, pl.ds(pl.multiple_of(chunk * 256, 256), 256)]
        for m in range(3):
            part_y[slot, pl.ds(m, 1), :] = jnp.sum(block * coarse[m], axis=0, keepdims=True)

    for k, place in in_plane:
        form_part(k, peer_at(place))
        spread_out(0, [(k, place)], lambda peer: part_y.at[k], lambda k: recv_y.at[k - 1])
    form_part(0, (gx, yz))
    assemble_sides(image)
    fold_y(image, 0, 2, 224)
    apply_to_image(0)
    wait_bytes(recv_y, red_recv.at[0])
    total = part_y[0]
    for k in range(PLANE - 1):
        total += recv_y[k]
    sum_b[...] = total
    spread_out(1, in_ring, lambda peer: sum_b, lambda k: recv_b.at[k - 1])
    apply_to_image(1)
    wait_bytes(recv_b, red_recv.at[1])
    total = sum_b[...]
    for k in range(RING - 1):
        total += recv_b[k]
    all_y[here] = total
    spread_out(2, in_plane, lambda peer: all_y.at[here], lambda k: all_y.at[here])
    apply_to_image(2)
    wait_bytes(all_y.at[pl.ds(0, PLANE - 1)], red_recv.at[2])

    sums = [jnp.zeros((32, 256), F32) for _ in range(3)]
    for j in range(PLANE):
        block = xxt[:, pl.ds(256 * j, 256)]
        for m in range(3):
            sums[m] += block * all_y[j, pl.ds(m, 1), :]
    for m in range(3):
        column = jnp.sum(sums[m], axis=1, keepdims=True)
        for b in range(4):
            line = jnp.sum(onehot[:, pl.ds(256 * b, 256)] * column, axis=0, keepdims=True)
            cblock[m, pl.ds(8 * b, 8), :] = jnp.broadcast_to(line, (8, 256))

    def add_correction(m, p):
        rows = rows_of(p)
        total = cblock[0] * grads[m, 0, rows, :]
        total += cblock[1] * grads[m, 1, rows, :]
        total += cblock[2] * grads[m, 2, rows, :]
        put(local2, m, rows, get(local2, m, rows) + total * (plane[0] * float(WEIGHTS[p])))

    for m in range(3):
        add_correction(m, 0)
        add_correction(m, 7)
        send_x(1, local2, m)
    send_corners(1, local2)
    for m in range(3):
        for p in range(1, 7):
            add_correction(m, p)
        send_y(1, local2, m)
    for m in range(3):
        for p in range(8):
            put(probe, m, rows_of(p), get(image, m, rows_of(p)) + cblock[m])

    def copies_out(source, target, n):
        copies = [
            pltpu.make_async_copy(
                source.at[:, h], target.at[:, :, pl.ds(128 * h, 128)], out_sem.at[n + h]
            )
            for h in range(2)
        ]
        for copy in copies:
            copy.start()
        return copies

    outs = copies_out(probe, probe_hbm, 0)
    for m in range(3):
        for p in range(1, 7):
            put(second, m, rows_of(p), fold_z(get(local2, m, rows_of(p))))

    def weighed(value, weights):
        return jnp.sum(jnp.sum(value * weights, axis=0, keepdims=True), axis=1, keepdims=True)

    inner = jnp.where((row32 % 8 == 0) | (row32 % 8 == 7), 0.0, plane[1])
    acc_in_sp, acc_in_pp, acc_pp = (jnp.zeros((32, 256), F32) for _ in range(3))
    for p in range(8):
        pp = jnp.zeros((32, 256), F32)
        for m in range(3):
            pr = get(probe, m, rows_of(p))
            pp += pr * pr
            if 0 < p < 7:
                acc_in_sp += get(second, m, rows_of(p)) * pr
        if 0 < p < 7:
            acc_in_pp += pp
        acc_pp += (0.5 if p in (0, 7) else 1.0) * pp
    in_sp, in_pp, pp = (
        weighed(acc_in_sp, inner),
        weighed(acc_in_pp, inner),
        weighed(acc_pp, plane[1]),
    )
    own = jnp.where(in_pp > 0, in_sp / jnp.where(in_pp > 0, in_pp, 1.0), 0.0)
    fold_y(second, 32, 6, 32)

    def residual_sums(places):
        q, rr = 0.0, 0.0
        for rows in places:
            for m in range(3):
                pr = get(probe, m, rows)
                rest = get(second, m, rows) - own * pr
                q += rest * pr
                rr += rest * rest
        return q, rr

    not_sides = jnp.where((row32 == 0) | (row32 == 31), 0.0, plane[1])
    sums_in = [v * not_sides for v in residual_sums([rows_of(p) for p in range(1, 7)])]

    wait_halo(1, halo_recv)
    assemble_planes(1, local2, second)
    assemble_sides(second)
    fold_y(second, 0, 2, 224)
    outs += copies_out(second, sec_hbm, 2)
    sums_faces = residual_sums([rows_of(0), rows_of(7)])
    sums_sides = residual_sums([pl.ds(32, 6, stride=32), pl.ds(63, 6, stride=32)])
    q, rr = (
        jnp.sum(
            jnp.sum(one + two * (0.5 * plane[1]), axis=0, keepdims=True)
            + jnp.sum(three, axis=0, keepdims=True) * plane[1, 0:1, :],
            axis=1,
            keepdims=True,
        )
        for one, two, three in zip(sums_in, sums_faces, sums_sides)
    )

    lane128 = lax.broadcasted_iota(jnp.int32, (1, 128), 1)

    def total_of(rows):
        return jnp.sum(rows, axis=0, keepdims=True)

    row_a[...] = jnp.where(
        lane128 < 32,
        own,
        jnp.where(lane128 < 64, q, jnp.where(lane128 < 96, pp, rr)),
    )
    spread_out(3, everyone, lambda peer: row_a, lambda k: recv_ra.at[pl.ds(k - 1, 1), :])
    recv_ra[pl.ds(255, 1), :] = row_a[...]
    wait_bytes(recv_ra.at[pl.ds(0, 255)], red_recv.at[3])
    own = recv_ra[...]
    q, pp, rr = (pltpu.roll(own, shift, 1) for shift in (96, 64, 32))
    weight_total = 343.0 * 128 * slabs * columns
    mean_sp, mean_pp = total_of(q + own * pp) / weight_total, total_of(pp) / weight_total
    coef = mean_sp / (mean_pp + epsilon)
    away = own - coef
    rest_mean = total_of(rr + 2.0 * away * q + away * away * pp) / weight_total
    rms = jnp.sqrt(jnp.maximum(rest_mean, 0.0) + epsilon)
    scal_ref[...] = jnp.concatenate([coef, rms, 1.0 / rms, jnp.zeros((5, 128), F32)], axis=0)

    wait_halo(0, halo_send)
    wait_halo(1, halo_send)
    wait_bytes(recv_y, red_send.at[0])
    wait_bytes(recv_b, red_send.at[1])
    wait_bytes(all_y.at[pl.ds(0, PLANE - 1)], red_send.at[2])
    wait_bytes(recv_ra.at[pl.ds(0, 255)], red_send.at[3])
    for out in outs:
        out.wait()


def normalise(second, probe, scal, basis_hbm, hess, basis, sems):
    coef, scale = scal[0:1, 0:1], scal[2:3, 0:1]
    hess[0] = scal[0, 0]
    hess[1] = scal[1, 0]
    stores = []
    for i in range(6):
        m, part = i // 2, pl.ds(128 * (i % 2), 128)
        for p in range(4):
            at = pl.ds(part.start + 32 * p, 32)
            basis[m, at, :] = (second[m, at, :] - coef * probe[m, at, :]) * scale
        stores.append(
            pltpu.make_async_copy(basis.at[m, part], basis_hbm.at[m, part], sems.at[i])
        )
        stores[-1].start()
    for store in stores:
        store.wait()


def shards(slabs, columns, state, direction, xxt_rows, coarse_ids):
    shape = state.shape
    ops = constants()
    vmem = pltpu.VMEM
    field = (3, 256, 256)
    halved = (3, 2, 256, 128)

    def body(*refs):
        kernel(slabs, columns, *refs)

    anywhere = pl.BlockSpec(memory_space=pl.ANY)
    sec, probe, scal = pl.pallas_call(
        body,
        out_shape=(
            jax.ShapeDtypeStruct(field, F32),
            jax.ShapeDtypeStruct(field, F32),
            jax.ShapeDtypeStruct((8, 128), F32),
        ),
        in_specs=[pl.BlockSpec(memory_space=pltpu.HBM)] * 5,
        out_specs=(anywhere, anywhere, pl.BlockSpec(memory_space=vmem)),
        scratch_shapes=[
            vmem(field, F32),
            vmem(field, F32),
            vmem((32, 8192), F32),
            vmem((1, 128), jnp.int32),
            vmem((896, 512), BF16),
            vmem((2, 32, 256), F32),
            vmem((2,) + field, BF16),
            vmem((2,) + field, BF16),
            vmem((3, 3, 256, 256), F32),
            vmem((3, 768, 256), F32),
            vmem((3, 2, 256, 256), F32),
            vmem(halved, F32),
            vmem(halved, F32),
            vmem(halved, F32),
            vmem(halved, F32),
            vmem(halved, F32),
            vmem((2, 3, 8, 256), F32),
            vmem((3, 32, 256), F32),
            vmem((32, 1024), F32),
            vmem((3, 32, 256), F32),
            vmem((PLANE, 4, 256), F32),
            vmem((PLANE - 1, 4, 256), F32),
            vmem((4, 256), F32),
            vmem((RING - 1, 4, 256), F32),
            vmem((PLANE, 4, 256), F32),
            vmem((2, 3, 8, 256), F32),
            vmem((2, 3, 8, 256), F32),
            vmem((2, 4, 4, 256), F32),
            vmem((2, 3, 2, 32, 128), F32),
            vmem((2, 3, 2, 32, 128), F32),
            vmem((2, 3, 8, 256), F32),
            vmem((2, 3, 8, 256), F32),
            vmem((2, 4, 4, 256), F32),
            vmem((1, 128), F32),
            vmem((256, 128), F32),
            pltpu.SemaphoreType.DMA((10,)),
            pltpu.SemaphoreType.DMA((4,)),
            pltpu.SemaphoreType.DMA((2, 8)),
            pltpu.SemaphoreType.DMA((2, 8)),
            pltpu.SemaphoreType.DMA((4,)),
            pltpu.SemaphoreType.DMA((4,)),
        ],
        compiler_params=pltpu.CompilerParams(
            collective_id=0, has_side_effects=True, vmem_limit_bytes=VMEM_LIMIT
        ),
        name="jacobian_products",
    )(
        state.reshape(field),
        direction.reshape(field),
        xxt_rows,
        coarse_ids,
        jnp.asarray(ops),
    )
    next_basis, hessenberg = pl.pallas_call(
        normalise,
        out_shape=(jax.ShapeDtypeStruct(field, F32), jax.ShapeDtypeStruct((2,), F32)),
        in_specs=[pl.BlockSpec(memory_space=vmem)] * 3,
        out_specs=(
            pl.BlockSpec(memory_space=pltpu.HBM),
            pl.BlockSpec(memory_space=pltpu.SMEM),
        ),
        scratch_shapes=[
            vmem(field, F32),
            pltpu.SemaphoreType.DMA((6,)),
        ],
        compiler_params=pltpu.CompilerParams(vmem_limit_bytes=16 * 1024 * 1024),
        name="normalise",
    )(sec, probe, scal)
    return next_basis.reshape(shape), hessenberg


def solution(mesh):
    slabs, columns = mesh.shape["gx"], mesh.shape["yz"]

    def local_shards(*args):
        return shards(slabs, columns, *args)

    return jax.shard_map(
        local_shards,
        mesh=mesh,
        in_specs=(
            P(None, "gx", "yz", None),
            P(None, "gx", "yz", None),
            P(("gx", "yz"), None),
            P(("gx", "yz"), None),
        ),
        out_specs=(P(None, "gx", "yz", None), P()),
        check_vma=False,
    )
```

```python
import jax
import jax.numpy as jnp
import ml_dtypes
import numpy as np
from jax import lax
from jax.experimental import pallas as pl
from jax.experimental.pallas import tpu as pltpu
from jax.sharding import PartitionSpec as P

viscosity = 0.05
epsilon = 1e-06
MESH = pl.DeviceIdType.MESH
F32 = jnp.float32
BF16 = jnp.bfloat16
PLANE = 32
RING = 8
VMEM_LIMIT = 52 * 1024 * 1024


def tables():
    points = np.array(
        [
            -1.0,
            -0.8717401485096066,
            -0.5917001814331423,
            -0.2092992179024789,
            0.2092992179024789,
            0.5917001814331423,
            0.8717401485096066,
            1.0,
        ]
    )
    weights = np.array(
        [
            1.0 / 28.0,
            0.2107042271435061,
            0.3411226924835044,
            0.4124587946587038,
            0.4124587946587038,
            0.3411226924835044,
            0.2107042271435061,
            1.0 / 28.0,
        ]
    )
    differ = points[:, None] - points[None, :]
    positions = np.arange(8)
    differ[positions, positions] = 1.0
    barycentric = 1.0 / np.prod(differ, axis=1)
    derivative = barycentric[None, :] / barycentric[:, None] / differ
    derivative[positions, positions] = 0.0
    derivative[positions, positions] = -derivative.sum(axis=1)
    return derivative, weights


X_ORDER = (0, 7, 1, 2, 3, 4, 5, 6)
GROUPS = ((0, 2, (0, 7)), (2, 8, (1, 2, 3, 4, 5, 6)))
DIMS = {"z": 8, "x": 4, "y": 4, "c": 2}


def offsets(names):
    found = []
    for k in range(1, int(np.prod([DIMS[n] for n in names]))):
        place, hops, rest = {}, 0.0, k
        for n in reversed(names):
            place[n] = rest % DIMS[n]
            rest //= DIMS[n]
            near = min(place[n], DIMS[n] - place[n])
            hops += 0.25 * near if n == "c" else near
        found.append((-hops, k, place))
    return [(k, place) for _, k, place in sorted(found, key=lambda item: item[:2])]


def halves(matrix):
    high = matrix.astype(ml_dtypes.bfloat16)
    low = (matrix - high.astype(np.float64)).astype(ml_dtypes.bfloat16)
    return high, low


def constants():
    derivative, weights = tables()
    stiff = viscosity * (derivative.T * weights[None, :]) @ derivative / weights[:, None]
    eye, order = np.eye, np.array(X_ORDER)
    derivative_x, stiff_x = (op[order][:, order] for op in (derivative, stiff))
    ops = [
        np.kron(derivative_x, eye(8)),
        np.kron(eye(8), derivative),
        np.kron(stiff_x, eye(8)) + np.kron(eye(8), stiff),
    ]
    left = [op[8 * start : 8 * end] for start, end, _ in GROUPS for op in ops]
    high, low = halves(np.concatenate(left, axis=0))
    right = np.concatenate([np.kron(eye(16), derivative.T), np.kron(eye(16), stiff.T)], axis=1)
    table = np.zeros((1024, 512), ml_dtypes.bfloat16)
    table[:192, :256] = np.concatenate([high, low, high, low], axis=1)
    table[192:320] = np.concatenate(halves(right), axis=1)
    return table


WEIGHTS = tables()[1]


def split(value):
    high = value.astype(BF16)
    return high, (value - high.astype(F32)).astype(BF16)


def kernel(
    slabs,
    columns,
    state_hbm,
    dir_hbm,
    xxt_hbm,
    ids_hbm,
    ops_hbm,
    sec_hbm,
    probe_hbm,
    scal_ref,
    state,
    direc,
    xxt,
    ids,
    left,
    right,
    plane,
    highs,
    lows,
    grads,
    lhs_out,
    rhs_out,
    local,
    image,
    local2,
    second,
    probe,
    ysides,
    tsum,
    onehot,
    cblock,
    part_y,
    recv_y,
    sum_b,
    recv_b,
    all_y,
    send_yl,
    send_yh,
    send_c,
    recv_xl,
    recv_xh,
    recv_yl,
    recv_yh,
    recv_c,
    row_a,
    recv_ra,
    in_sem,
    out_sem,
    halo_send,
    halo_recv,
    red_send,
    red_recv,
):
    gx, yz = lax.axis_index("gx"), lax.axis_index("yz")
    gz, px = gx // 4, gx % 4
    here = px * columns + yz

    z_at = [jnp.bitwise_and(gz + k, 7) * 4 for k in range(8)]
    x_at = [jnp.bitwise_and(px + k, 3) for k in range(4)]
    y_at = [jnp.bitwise_and(yz // 2 + k, 3) * 2 for k in range(4)]
    c_at = [jnp.bitwise_and(yz + k, 1) for k in range(2)]

    def peer_at(place):
        z, x, y, c = (place.get(name, 0) for name in "zxyc")
        return (z_at[z] + x_at[x], y_at[y] + c_at[c])

    in_plane, in_ring, everyone = offsets("xyc"), offsets("z"), offsets("zxyc")

    def beside(dx, dy):
        return (lax.rem(gx + dx + slabs, slabs), lax.rem(yz + dy + columns, columns))

    pairs = [(ops_hbm.at[pl.ds(0, 192), pl.ds(0, 256)], left)]
    pairs += [(ops_hbm.at[pl.ds(192, 128)], right)]
    pairs += [(state_hbm.at[m], state.at[m]) for m in range(3)]
    pairs += [(dir_hbm.at[m], direc.at[m]) for m in range(3)]
    pairs += [(ids_hbm, ids), (xxt_hbm, xxt)]
    loads = [pltpu.make_async_copy(src, dst, in_sem.at[i]) for i, (src, dst) in enumerate(pairs)]
    for load in loads[:-1]:
        load.start()

    barrier = pltpu.get_barrier_semaphore()
    greeted = [peer_at(place) for _, place in in_ring + in_plane]
    greeted += [beside(dx, dy) for dx in (-1, 1) for dy in (-1, 0, 1)]
    for peer in greeted:
        pl.semaphore_signal(barrier, inc=1, device_id=peer, device_id_type=MESH)

    lane = lax.broadcasted_iota(jnp.int32, (1, 256), 1)
    from_next = ((lane % 8 == 7) & (lane != 255)).astype(F32)
    from_last = ((lane % 8 == 0) & (lane != 0)).astype(F32)
    inside = ((lane != 0) & (lane != 255)).astype(F32)

    def by_place(place, values):
        place = place % 8
        place = jnp.minimum(place, 7 - place)
        result = jnp.full(place.shape, values[0], F32)
        for i in range(1, 4):
            result = jnp.where(place == i, float(values[i]), result)
        return result

    row32 = lax.broadcasted_iota(jnp.int32, (32, 1), 0)
    half = (0.5, 1.0, 1.0, 1.0)
    weights4 = [float(w) for w in WEIGHTS[:4]]
    plane[0] = by_place(row32, weights4) * by_place(lane, weights4)
    plane[1] = by_place(row32, half) * by_place(lane, half)
    wall_xl = jnp.where(gx == 0, 0.0, 1.0).astype(F32)
    wall_xh = jnp.where(gx == slabs - 1, 0.0, 1.0).astype(F32)
    wall_yl = jnp.where(yz == 0, 0.0, 1.0).astype(F32)
    wall_yh = jnp.where(yz == columns - 1, 0.0, 1.0).astype(F32)
    row8 = lax.broadcasted_iota(jnp.int32, (8, 1), 0)
    wall_x = jnp.where(row8 == 0, wall_xl, jnp.where(row8 == 7, wall_xh, 1.0))

    def fold_z(value):
        return (
            value * inside
            + pltpu.roll(value, 255, 1) * from_next
            + pltpu.roll(value, 1, 1) * from_last
        )

    def rows_of(p):
        return pl.ds(32 * p, 32)

    def get(ref, m, rows):
        return jnp.concatenate([ref[m, 0, rows, :], ref[m, 1, rows, :]], axis=1)

    def put(ref, m, rows, value):
        ref[m, 0, rows, :] = value[:, :128]
        ref[m, 1, rows, :] = value[:, 128:]

    def whole(ref, m, rows):
        return ref[m, rows, :]

    def places_of(g, b):
        start, end, _ = GROUPS[g]
        return [(8 * (i - start), pl.ds(32 * X_ORDER[i] + 8 * b, 8)) for i in range(start, end)]

    def split_into(take, vector, which, m):
        for b in range(4):
            pieces = [take(vector, m, pl.ds(32 * x + 8 * b, 8)) for x in X_ORDER]
            high, low = split(jnp.concatenate(pieces, axis=0))
            highs[which, m, b] = high
            lows[which, m, b] = low

    def products_left(which, m, b, g, count):
        start, size = ((0, 16), (48, 48))[g]
        high, low = highs[which, m, b], lows[which, m, b]
        return jnp.dot(
            left[pl.ds(start, size * count), :],
            jnp.concatenate([high, high, low, low], axis=0),
            preferred_element_type=F32,
        )

    def products_right(which, m, g, cols):
        high, low = (right[:, pl.ds(start, cols)] for start in (0, 256))
        ops = jnp.concatenate([high, low, high], axis=0)
        rows = (pl.ds(0, 16), pl.ds(16, 48))[g]
        results = []
        for h in range(2):
            high, low = (
                jnp.concatenate(
                    [ref[which, m, b, rows, pl.ds(128 * h, 128)] for b in range(4)], axis=0
                )
                for ref in (highs, lows)
            )
            both = jnp.concatenate([high, high, low], axis=1)
            results.append(jnp.dot(both, ops, preferred_element_type=F32))
        return results

    def state_gradients(m, g):
        size = (16, 48)[g]
        one, two = products_right(0, m, g, 128)
        for b in range(4):
            by_left = products_left(0, m, b, g, 2)
            for at, rows in places_of(g, b):
                for op in range(2):
                    grads[m, op, rows, :] = by_left[size * op + at : size * op + at + 8]
                at += size * b
                grads[m, 2, rows, :] = jnp.concatenate([one[at : at + 8], two[at : at + 8]], axis=1)

    def multiply(which, m, g):
        size = (16, 48)[g]
        by_right = products_right(which, m, g, 256)
        for b in range(4):
            by_left = products_left(which, m, b, g, 3)
            for at, rows in places_of(g, b):
                for op in range(3):
                    lhs_out[m, op, rows, :] = by_left[size * op + at : size * op + at + 8]
                at += size * b
                for h in range(2):
                    rhs_out[m, h, rows, :] = by_right[h][at : at + 8]

    def along_z(m, rows, kind):
        part = pl.ds(128 * kind, 128)
        return jnp.concatenate([rhs_out[m, 0, rows, part], rhs_out[m, 1, rows, part]], axis=1)

    def combine(vector, take, m, g, target):
        for p in GROUPS[g][2]:
            rows = rows_of(p)
            total = lhs_out[m, 2, rows, :] + along_z(m, rows, 1)
            total += state[0, rows, :] * lhs_out[m, 0, rows, :]
            total += state[1, rows, :] * lhs_out[m, 1, rows, :]
            total += state[2, rows, :] * along_z(m, rows, 0)
            for k in range(3):
                total += take(vector, k, rows) * grads[m, k, rows, :]
            put(target, m, rows, total * (plane[0] * float(WEIGHTS[p])))

    def apply_to_image(m):
        split_into(get, image, 1, m)
        for g in range(2):
            multiply(1, m, g)
            combine(image, get, m, g, local2)

    def send(turn, index, src, dst, peer):
        pltpu.make_async_remote_copy(
            src_ref=src,
            dst_ref=dst,
            send_sem=halo_send.at[turn, index],
            recv_sem=halo_recv.at[turn, index],
            device_id=peer,
            device_id_type=MESH,
        ).start()

    def send_x(turn, source, m):
        send(turn, 0, source.at[m, :, pl.ds(224, 32), :], recv_xl.at[turn, m], beside(1, 0))
        send(turn, 1, source.at[m, :, pl.ds(0, 32), :], recv_xh.at[turn, m], beside(-1, 0))

    def send_corners(turn, source):
        for m in range(3):
            for i, row in enumerate((0, 31, 224, 255)):
                send_c[turn, i, pl.ds(m, 1), :] = get(source, m, pl.ds(row, 1))
        for i, (dx, dy) in enumerate(((-1, -1), (-1, 1), (1, -1), (1, 1))):
            send(turn, 4 + i, send_c.at[turn, i], recv_c.at[turn, i], beside(dx, dy))

    def send_y(turn, source, m):
        send_yl[turn, m] = get(source, m, pl.ds(0, 8, stride=32))
        send_yh[turn, m] = get(source, m, pl.ds(31, 8, stride=32))
        send(turn, 2, send_yh.at[turn, m], recv_yl.at[turn, m], beside(0, 1))
        send(turn, 3, send_yl.at[turn, m], recv_yh.at[turn, m], beside(0, -1))

    def halo_refs(turn):
        refs = [recv_xl.at[turn], recv_xh.at[turn], recv_yl.at[turn], recv_yh.at[turn]]
        return refs + [recv_c.at[turn, i] for i in range(4)]

    def wait_halo(turn, sems):
        for i, ref in enumerate(halo_refs(turn)):
            pltpu.make_async_copy(ref, ref, sems.at[turn, i]).wait()

    def fold_y(target, first, count, stride):
        for m in range(3):
            for b in range(3):
                one = pl.ds(first + 8 * b + 7, count, stride=stride)
                two = pl.ds(first + 8 * b + 8, count, stride=stride)
                both = get(target, m, one) + get(target, m, two)
                put(target, m, one, both)
                put(target, m, two, both)

    def assemble_planes(turn, source, target):
        for m in range(3):
            value = get(source, m, rows_of(0)) + get(recv_xl.at[turn], m, pl.ds(0, 32))
            put(target, m, rows_of(0), fold_z(value * wall_xl))
            value = get(source, m, rows_of(7)) + get(recv_xh.at[turn], m, pl.ds(0, 32))
            put(target, m, rows_of(7), fold_z(value * wall_xh))
            at_m = pl.ds(m, 1)
            low = recv_yl[turn, m]
            low += jnp.where(row8 == 0, recv_c[turn, 3, at_m, :], 0.0)
            low += jnp.where(row8 == 7, recv_c[turn, 1, at_m, :], 0.0)
            high = recv_yh[turn, m]
            high += jnp.where(row8 == 0, recv_c[turn, 2, at_m, :], 0.0)
            high += jnp.where(row8 == 7, recv_c[turn, 0, at_m, :], 0.0)
            ysides[0, m] = fold_z(low) * wall_x
            ysides[1, m] = fold_z(high) * wall_x

    def assemble_sides(target):
        first, last = pl.ds(0, 8, stride=32), pl.ds(31, 8, stride=32)
        for m in range(3):
            put(target, m, first, (get(target, m, first) + ysides[0, m]) * wall_yl)
            put(target, m, last, (get(target, m, last) + ysides[1, m]) * wall_yh)

    def spread_out(phase, places, src_of, dst_of):
        for k, place in places:
            peer = peer_at(place)
            pltpu.make_async_remote_copy(
                src_ref=src_of(peer),
                dst_ref=dst_of(k),
                send_sem=red_send.at[phase],
                recv_sem=red_recv.at[phase],
                device_id=peer,
                device_id_type=MESH,
            ).start()

    def wait_bytes(ref, sem):
        pltpu.make_async_copy(ref, ref, sem).wait()

    loads[0].wait()
    loads[1].wait()
    for m in range(3):
        loads[2 + m].wait()
        split_into(whole, state, 0, m)
        state_gradients(m, 0)
    for m in range(3):
        loads[5 + m].wait()
        split_into(whole, direc, 1, m)
    for m in range(3):
        multiply(1, m, 0)
        combine(direc, whole, m, 0, local)
        if m == 0:
            pl.semaphore_wait(barrier, len(greeted))
        send_x(0, local, m)
    send_corners(0, local)
    loads[9].start()
    for m in range(3):
        state_gradients(m, 1)
        multiply(1, m, 1)
        combine(direc, whole, m, 1, local)
        send_y(0, local, m)
    for m in range(3):
        total = jnp.zeros((32, 256), F32)
        for p in range(1, 7):
            value = fold_z(get(local, m, rows_of(p)))
            put(image, m, rows_of(p), value)
            total += float(WEIGHTS[p]) * value
        tsum[m] = total
    fold_y(image, 32, 6, 32)

    loads[8].wait()
    elem = lax.broadcasted_iota(jnp.int32, (128, 1024), 0)
    spot = lax.broadcasted_iota(jnp.int32, (128, 1024), 1)
    wide = jnp.dot(
        jnp.broadcast_to(ids[...].astype(F32), (8, 128)).astype(BF16),
        (spot // 8 == elem).astype(F32).astype(BF16),
        preferred_element_type=F32,
    )
    for t in range(4):
        row = (lax.broadcasted_iota(jnp.int32, (8, 1024), 0) + 8 * t).astype(F32)
        onehot[pl.ds(8 * t, 8), :] = jnp.where(jnp.abs(wide - row) < 0.5, 1.0, 0.0)
    loads[9].wait()

    wait_halo(0, halo_recv)
    assemble_planes(0, local, image)

    weight8 = by_place(row8, weights4)
    y_next = ((row32 % 8 == 7) & (row32 != 31)).astype(F32)
    y_last = ((row32 % 8 == 0) & (row32 != 0)).astype(F32)
    wall_y = jnp.where(row32 == 0, wall_yl, jnp.where(row32 == 31, wall_yh, 1.0))
    coarse = []
    for m in range(3):
        total = tsum[m] + float(WEIGHTS[0]) * (get(image, m, rows_of(0)) + get(image, m, rows_of(7)))
        low, high = (
            jnp.sum(ysides[i, m] * weight8, axis=0, keepdims=True) for i in range(2)
        )
        total += jnp.where(row32 == 0, low, 0.0) + jnp.where(row32 == 31, high, 0.0)
        folded = total + pltpu.roll(total, 31, 0) * y_next + pltpu.roll(total, 1, 0) * y_last
        folded *= plane[0] * wall_y
        acc = jnp.zeros((32, 256), F32)
        for b in range(4):
            line = jnp.sum(folded[8 * b : 8 * b + 8], axis=0, keepdims=True)
            acc += onehot[:, pl.ds(256 * b, 256)] * line
        coarse.append(jnp.sum(acc, axis=1, keepdims=True))

    def form_part(slot, peer):
        chunk = lax.rem(peer[0], 4) * columns + peer[1]
        block = xxt[:, pl.ds(pl.multiple_of(chunk * 256, 256), 256)]
        for m in range(3):
            part_y[slot, pl.ds(m, 1), :] = jnp.sum(block * coarse[m], axis=0, keepdims=True)

    for k, place in in_plane:
        form_part(k, peer_at(place))
        spread_out(0, [(k, place)], lambda peer: part_y.at[k], lambda k: recv_y.at[k - 1])
    form_part(0, (gx, yz))
    assemble_sides(image)
    fold_y(image, 0, 2, 224)
    apply_to_image(0)
    wait_bytes(recv_y, red_recv.at[0])
    total = part_y[0]
    for k in range(PLANE - 1):
        total += recv_y[k]
    sum_b[...] = total
    spread_out(1, in_ring, lambda peer: sum_b, lambda k: recv_b.at[k - 1])
    apply_to_image(1)
    wait_bytes(recv_b, red_recv.at[1])
    total = sum_b[...]
    for k in range(RING - 1):
        total += recv_b[k]
    all_y[here] = total
    spread_out(2, in_plane, lambda peer: all_y.at[here], lambda k: all_y.at[here])
    apply_to_image(2)
    wait_bytes(all_y.at[pl.ds(0, PLANE - 1)], red_recv.at[2])

    sums = [jnp.zeros((32, 256), F32) for _ in range(3)]
    for j in range(PLANE):
        block = xxt[:, pl.ds(256 * j, 256)]
        for m in range(3):
            sums[m] += block * all_y[j, pl.ds(m, 1), :]
    for m in range(3):
        column = jnp.sum(sums[m], axis=1, keepdims=True)
        for b in range(4):
            line = jnp.sum(onehot[:, pl.ds(256 * b, 256)] * column, axis=0, keepdims=True)
            cblock[m, pl.ds(8 * b, 8), :] = jnp.broadcast_to(line, (8, 256))

    def add_correction(m, p):
        rows = rows_of(p)
        total = cblock[0] * grads[m, 0, rows, :]
        total += cblock[1] * grads[m, 1, rows, :]
        total += cblock[2] * grads[m, 2, rows, :]
        put(local2, m, rows, get(local2, m, rows) + total * (plane[0] * float(WEIGHTS[p])))

    for m in range(3):
        add_correction(m, 0)
        add_correction(m, 7)
        send_x(1, local2, m)
    send_corners(1, local2)
    for m in range(3):
        for p in range(1, 7):
            add_correction(m, p)
        send_y(1, local2, m)
    for m in range(3):
        for p in range(8):
            put(probe, m, rows_of(p), get(image, m, rows_of(p)) + cblock[m])

    def copies_out(source, target, n):
        copies = [
            pltpu.make_async_copy(
                source.at[:, h], target.at[:, :, pl.ds(128 * h, 128)], out_sem.at[n + h]
            )
            for h in range(2)
        ]
        for copy in copies:
            copy.start()
        return copies

    outs = copies_out(probe, probe_hbm, 0)
    for m in range(3):
        for p in range(1, 7):
            put(second, m, rows_of(p), fold_z(get(local2, m, rows_of(p))))

    def weighed(value, weights):
        return jnp.sum(jnp.sum(value * weights, axis=0, keepdims=True), axis=1, keepdims=True)

    inner = jnp.where((row32 % 8 == 0) | (row32 % 8 == 7), 0.0, plane[1])
    acc_in_sp, acc_in_pp, acc_pp = (jnp.zeros((32, 256), F32) for _ in range(3))
    for p in range(8):
        pp = jnp.zeros((32, 256), F32)
        for m in range(3):
            pr = get(probe, m, rows_of(p))
            pp += pr * pr
            if 0 < p < 7:
                acc_in_sp += get(second, m, rows_of(p)) * pr
        if 0 < p < 7:
            acc_in_pp += pp
        acc_pp += (0.5 if p in (0, 7) else 1.0) * pp
    in_sp, in_pp, pp = (
        weighed(acc_in_sp, inner),
        weighed(acc_in_pp, inner),
        weighed(acc_pp, plane[1]),
    )
    own = jnp.where(in_pp > 0, in_sp / jnp.where(in_pp > 0, in_pp, 1.0), 0.0)
    fold_y(second, 32, 6, 32)

    def residual_sums(places):
        q, rr = 0.0, 0.0
        for rows in places:
            for m in range(3):
                pr = get(probe, m, rows)
                rest = get(second, m, rows) - own * pr
                q += rest * pr
                rr += rest * rest
        return q, rr

    not_sides = jnp.where((row32 == 0) | (row32 == 31), 0.0, plane[1])
    sums_in = [v * not_sides for v in residual_sums([rows_of(p) for p in range(1, 7)])]

    wait_halo(1, halo_recv)
    assemble_planes(1, local2, second)
    assemble_sides(second)
    fold_y(second, 0, 2, 224)
    outs += copies_out(second, sec_hbm, 2)
    sums_faces = residual_sums([rows_of(0), rows_of(7)])
    sums_sides = residual_sums([pl.ds(32, 6, stride=32), pl.ds(63, 6, stride=32)])
    q, rr = (
        jnp.sum(
            jnp.sum(one + two * (0.5 * plane[1]), axis=0, keepdims=True)
            + jnp.sum(three, axis=0, keepdims=True) * plane[1, 0:1, :],
            axis=1,
            keepdims=True,
        )
        for one, two, three in zip(sums_in, sums_faces, sums_sides)
    )

    lane128 = lax.broadcasted_iota(jnp.int32, (1, 128), 1)

    def total_of(rows):
        return jnp.sum(rows, axis=0, keepdims=True)

    row_a[...] = jnp.where(
        lane128 < 32,
        own,
        jnp.where(lane128 < 64, q, jnp.where(lane128 < 96, pp, rr)),
    )
    spread_out(3, everyone, lambda peer: row_a, lambda k: recv_ra.at[pl.ds(k - 1, 1), :])
    recv_ra[pl.ds(255, 1), :] = row_a[...]
    wait_bytes(recv_ra.at[pl.ds(0, 255)], red_recv.at[3])
    own = recv_ra[...]
    q, pp, rr = (pltpu.roll(own, shift, 1) for shift in (96, 64, 32))
    weight_total = 343.0 * 128 * slabs * columns
    mean_sp, mean_pp = total_of(q + own * pp) / weight_total, total_of(pp) / weight_total
    coef = mean_sp / (mean_pp + epsilon)
    away = own - coef
    rest_mean = total_of(rr + 2.0 * away * q + away * away * pp) / weight_total
    rms = jnp.sqrt(jnp.maximum(rest_mean, 0.0) + epsilon)
    scal_ref[...] = jnp.concatenate([coef, rms, 1.0 / rms, jnp.zeros((5, 128), F32)], axis=0)

    wait_halo(0, halo_send)
    wait_halo(1, halo_send)
    wait_bytes(recv_y, red_send.at[0])
    wait_bytes(recv_b, red_send.at[1])
    wait_bytes(all_y.at[pl.ds(0, PLANE - 1)], red_send.at[2])
    wait_bytes(recv_ra.at[pl.ds(0, 255)], red_send.at[3])
    for out in outs:
        out.wait()


def normalise(second, probe, scal, basis_hbm, hess, basis, sems):
    coef, scale = scal[0:1, 0:1], scal[2:3, 0:1]
    hess[0] = scal[0, 0]
    hess[1] = scal[1, 0]
    stores = []
    for i in range(6):
        m, part = i // 2, pl.ds(128 * (i % 2), 128)
        for p in range(4):
            at = pl.ds(part.start + 32 * p, 32)
            basis[m, at, :] = (second[m, at, :] - coef * probe[m, at, :]) * scale
        stores.append(
            pltpu.make_async_copy(basis.at[m, part], basis_hbm.at[m, part], sems.at[i])
        )
        stores[-1].start()
    for store in stores:
        store.wait()


def shards(slabs, columns, state, direction, xxt_rows, coarse_ids):
    shape = state.shape
    ops = constants()
    vmem = pltpu.VMEM
    field = (3, 256, 256)
    halved = (3, 2, 256, 128)

    def body(*refs):
        kernel(slabs, columns, *refs)

    anywhere = pl.BlockSpec(memory_space=pl.ANY)
    sec, probe, scal = pl.pallas_call(
        body,
        out_shape=(
            jax.ShapeDtypeStruct(field, F32),
            jax.ShapeDtypeStruct(field, F32),
            jax.ShapeDtypeStruct((8, 128), F32),
        ),
        in_specs=[pl.BlockSpec(memory_space=pltpu.HBM)] * 5,
        out_specs=(anywhere, anywhere, pl.BlockSpec(memory_space=vmem)),
        scratch_shapes=[
            vmem(field, F32),
            vmem(field, F32),
            vmem((32, 8192), F32),
            vmem((1, 128), jnp.int32),
            vmem((192, 256), BF16),
            vmem((128, 512), BF16),
            vmem((2, 32, 256), F32),
            vmem((2, 3, 4, 64, 256), BF16),
            vmem((2, 3, 4, 64, 256), BF16),
            vmem((3, 3, 256, 256), F32),
            vmem((3, 3, 256, 256), F32),
            vmem((3, 2, 256, 256), F32),
            vmem(halved, F32),
            vmem(halved, F32),
            vmem(halved, F32),
            vmem(halved, F32),
            vmem(halved, F32),
            vmem((2, 3, 8, 256), F32),
            vmem((3, 32, 256), F32),
            vmem((32, 1024), F32),
            vmem((3, 32, 256), F32),
            vmem((PLANE, 4, 256), F32),
            vmem((PLANE - 1, 4, 256), F32),
            vmem((4, 256), F32),
            vmem((RING - 1, 4, 256), F32),
            vmem((PLANE, 4, 256), F32),
            vmem((2, 3, 8, 256), F32),
            vmem((2, 3, 8, 256), F32),
            vmem((2, 4, 4, 256), F32),
            vmem((2, 3, 2, 32, 128), F32),
            vmem((2, 3, 2, 32, 128), F32),
            vmem((2, 3, 8, 256), F32),
            vmem((2, 3, 8, 256), F32),
            vmem((2, 4, 4, 256), F32),
            vmem((1, 128), F32),
            vmem((256, 128), F32),
            pltpu.SemaphoreType.DMA((10,)),
            pltpu.SemaphoreType.DMA((4,)),
            pltpu.SemaphoreType.DMA((2, 8)),
            pltpu.SemaphoreType.DMA((2, 8)),
            pltpu.SemaphoreType.DMA((4,)),
            pltpu.SemaphoreType.DMA((4,)),
        ],
        compiler_params=pltpu.CompilerParams(
            collective_id=0, has_side_effects=True, vmem_limit_bytes=VMEM_LIMIT
        ),
        name="jacobian_products",
    )(
        state.reshape(field),
        direction.reshape(field),
        xxt_rows,
        coarse_ids,
        jnp.asarray(ops),
    )
    next_basis, hessenberg = pl.pallas_call(
        normalise,
        out_shape=(jax.ShapeDtypeStruct(field, F32), jax.ShapeDtypeStruct((2,), F32)),
        in_specs=[pl.BlockSpec(memory_space=vmem)] * 3,
        out_specs=(
            pl.BlockSpec(memory_space=pltpu.HBM),
            pl.BlockSpec(memory_space=pltpu.SMEM),
        ),
        scratch_shapes=[
            vmem(field, F32),
            pltpu.SemaphoreType.DMA((6,)),
        ],
        compiler_params=pltpu.CompilerParams(vmem_limit_bytes=16 * 1024 * 1024),
        name="normalise",
    )(sec, probe, scal)
    return next_basis.reshape(shape), hessenberg


def solution(mesh):
    slabs, columns = mesh.shape["gx"], mesh.shape["yz"]

    def local_shards(*args):
        return shards(slabs, columns, *args)

    return jax.shard_map(
        local_shards,
        mesh=mesh,
        in_specs=(
            P(None, "gx", "yz", None),
            P(None, "gx", "yz", None),
            P(("gx", "yz"), None),
            P(("gx", "yz"), None),
        ),
        out_specs=(P(None, "gx", "yz", None), P()),
        check_vma=False,
    )
```

```python
import jax
import jax.numpy as jnp
import ml_dtypes
import numpy as np
from jax import lax
from jax.experimental import pallas as pl
from jax.experimental.pallas import tpu as pltpu
from jax.sharding import PartitionSpec as P

viscosity = 0.05
epsilon = 1e-06
MESH = pl.DeviceIdType.MESH
F32 = jnp.float32
BF16 = jnp.bfloat16
PLANE = 32
RING = 8
VMEM_LIMIT = 52 * 1024 * 1024


def tables():
    points = np.array(
        [
            -1.0,
            -0.8717401485096066,
            -0.5917001814331423,
            -0.2092992179024789,
            0.2092992179024789,
            0.5917001814331423,
            0.8717401485096066,
            1.0,
        ]
    )
    weights = np.array(
        [
            1.0 / 28.0,
            0.2107042271435061,
            0.3411226924835044,
            0.4124587946587038,
            0.4124587946587038,
            0.3411226924835044,
            0.2107042271435061,
            1.0 / 28.0,
        ]
    )
    differ = points[:, None] - points[None, :]
    positions = np.arange(8)
    differ[positions, positions] = 1.0
    barycentric = 1.0 / np.prod(differ, axis=1)
    derivative = barycentric[None, :] / barycentric[:, None] / differ
    derivative[positions, positions] = 0.0
    derivative[positions, positions] = -derivative.sum(axis=1)
    return derivative, weights


X_ORDER = (0, 7, 1, 2, 3, 4, 5, 6)
GROUPS = ((0, 2, (0, 7)), (2, 8, (1, 2, 3, 4, 5, 6)))
DIMS = {"z": 8, "x": 4, "y": 4, "c": 2}


def offsets(names):
    found = []
    for k in range(1, int(np.prod([DIMS[n] for n in names]))):
        place, hops, rest = {}, 0.0, k
        for n in reversed(names):
            place[n] = rest % DIMS[n]
            rest //= DIMS[n]
            near = min(place[n], DIMS[n] - place[n])
            hops += 0.25 * near if n == "c" else near
        found.append((-hops, k, place))
    return [(k, place) for _, k, place in sorted(found, key=lambda item: item[:2])]


def halves(matrix):
    high = matrix.astype(ml_dtypes.bfloat16)
    low = (matrix - high.astype(np.float64)).astype(ml_dtypes.bfloat16)
    return high, low


def constants():
    derivative, weights = tables()
    stiff = viscosity * (derivative.T * weights[None, :]) @ derivative / weights[:, None]
    eye, order = np.eye, np.array(X_ORDER)
    derivative_x, stiff_x = (op[order][:, order] for op in (derivative, stiff))
    ops = [
        np.kron(derivative_x, eye(8)),
        np.kron(eye(8), derivative),
        np.kron(stiff_x, eye(8)) + np.kron(eye(8), stiff),
    ]
    left = [op[8 * start : 8 * end] for start, end, _ in GROUPS for op in ops]
    high, low = halves(np.concatenate(left, axis=0))
    right = np.concatenate([np.kron(eye(16), derivative.T), np.kron(eye(16), stiff.T)], axis=1)
    table = np.zeros((1024, 512), ml_dtypes.bfloat16)
    table[:192, :256] = np.concatenate([high, low, high, low], axis=1)
    table[192:320] = np.concatenate(halves(right), axis=1)
    return table


WEIGHTS = tables()[1]


def split(value):
    high = value.astype(BF16)
    return high, (value - high.astype(F32)).astype(BF16)


def kernel(
    slabs,
    columns,
    state_hbm,
    dir_hbm,
    xxt_hbm,
    ids_hbm,
    ops_hbm,
    sec_hbm,
    probe_hbm,
    scal_ref,
    state,
    direc,
    xxt,
    ids,
    left,
    right,
    plane,
    highs,
    lows,
    grads,
    lhs_out,
    rhs_out,
    local,
    image,
    local2,
    second,
    probe,
    ysides,
    tsum,
    onehot,
    cblock,
    part_y,
    recv_y,
    sum_b,
    recv_b,
    all_y,
    send_yl,
    send_yh,
    send_c,
    recv_xl,
    recv_xh,
    recv_yl,
    recv_yh,
    recv_c,
    row_a,
    recv_ra,
    in_sem,
    out_sem,
    halo_send,
    halo_recv,
    red_send,
    red_recv,
):
    gx, yz = lax.axis_index("gx"), lax.axis_index("yz")
    gz, px = gx // 4, gx % 4
    here = px * columns + yz

    z_at = [jnp.bitwise_and(gz + k, 7) * 4 for k in range(8)]
    x_at = [jnp.bitwise_and(px + k, 3) for k in range(4)]
    y_at = [jnp.bitwise_and(yz // 2 + k, 3) * 2 for k in range(4)]
    c_at = [jnp.bitwise_and(yz + k, 1) for k in range(2)]

    def peer_at(place):
        z, x, y, c = (place.get(name, 0) for name in "zxyc")
        return (z_at[z] + x_at[x], y_at[y] + c_at[c])

    in_plane, in_ring, everyone = offsets("xyc"), offsets("z"), offsets("zxyc")

    def beside(dx, dy):
        return (lax.rem(gx + dx + slabs, slabs), lax.rem(yz + dy + columns, columns))

    barrier = pltpu.get_barrier_semaphore()
    greeted = [peer_at(place) for _, place in in_plane + in_ring]
    greeted += [beside(dx, dy) for dx in (-1, 1) for dy in (-1, 0, 1)]
    for peer in greeted:
        pl.semaphore_signal(barrier, inc=1, device_id=peer, device_id_type=MESH)

    pairs = [(ops_hbm.at[pl.ds(0, 192), pl.ds(0, 256)], left)]
    pairs += [(ops_hbm.at[pl.ds(192, 128)], right)]
    pairs += [(state_hbm.at[m], state.at[m]) for m in range(3)]
    pairs += [(dir_hbm.at[m], direc.at[m]) for m in range(3)]
    pairs += [(ids_hbm, ids), (xxt_hbm, xxt)]
    loads = [pltpu.make_async_copy(src, dst, in_sem.at[i]) for i, (src, dst) in enumerate(pairs)]
    for load in loads[:-1]:
        load.start()

    lane = lax.broadcasted_iota(jnp.int32, (1, 256), 1)
    from_next = ((lane % 8 == 7) & (lane != 255)).astype(F32)
    from_last = ((lane % 8 == 0) & (lane != 0)).astype(F32)
    inside = ((lane != 0) & (lane != 255)).astype(F32)

    def by_place(place, values):
        place = place % 8
        place = jnp.minimum(place, 7 - place)
        result = jnp.full(place.shape, values[0], F32)
        for i in range(1, 4):
            result = jnp.where(place == i, float(values[i]), result)
        return result

    row32 = lax.broadcasted_iota(jnp.int32, (32, 1), 0)
    half = (0.5, 1.0, 1.0, 1.0)
    weights4 = [float(w) for w in WEIGHTS[:4]]
    plane[0] = by_place(row32, weights4) * by_place(lane, weights4)
    plane[1] = by_place(row32, half) * by_place(lane, half)
    wall_xl = jnp.where(gx == 0, 0.0, 1.0).astype(F32)
    wall_xh = jnp.where(gx == slabs - 1, 0.0, 1.0).astype(F32)
    wall_yl = jnp.where(yz == 0, 0.0, 1.0).astype(F32)
    wall_yh = jnp.where(yz == columns - 1, 0.0, 1.0).astype(F32)
    row8 = lax.broadcasted_iota(jnp.int32, (8, 1), 0)
    wall_x = jnp.where(row8 == 0, wall_xl, jnp.where(row8 == 7, wall_xh, 1.0))

    def fold_z(value):
        return (
            value * inside
            + pltpu.roll(value, 255, 1) * from_next
            + pltpu.roll(value, 1, 1) * from_last
        )

    def rows_of(p):
        return pl.ds(32 * p, 32)

    def get(ref, m, rows):
        return jnp.concatenate([ref[m, 0, rows, :], ref[m, 1, rows, :]], axis=1)

    def put(ref, m, rows, value):
        ref[m, 0, rows, :] = value[:, :128]
        ref[m, 1, rows, :] = value[:, 128:]

    def whole(ref, m, rows):
        return ref[m, rows, :]

    def places_of(g, b):
        start, end, _ = GROUPS[g]
        return [(8 * (i - start), pl.ds(32 * X_ORDER[i] + 8 * b, 8)) for i in range(start, end)]

    def split_into(take, vector, which, m):
        for b in range(4):
            pieces = [take(vector, m, pl.ds(32 * x + 8 * b, 8)) for x in X_ORDER]
            high, low = split(jnp.concatenate(pieces, axis=0))
            highs[which, m, b] = high
            lows[which, m, b] = low

    def products_left(which, m, b, g, count):
        start, size = ((0, 16), (48, 48))[g]
        high, low = highs[which, m, b], lows[which, m, b]
        return jnp.dot(
            left[pl.ds(start, size * count), :],
            jnp.concatenate([high, high, low, low], axis=0),
            preferred_element_type=F32,
        )

    def products_right(which, m, g, cols):
        high, low = (right[:, pl.ds(start, cols)] for start in (0, 256))
        ops = jnp.concatenate([high, low, high], axis=0)
        rows = (pl.ds(0, 16), pl.ds(16, 48))[g]
        results = []
        for h in range(2):
            high, low = (
                jnp.concatenate(
                    [ref[which, m, b, rows, pl.ds(128 * h, 128)] for b in range(4)], axis=0
                )
                for ref in (highs, lows)
            )
            both = jnp.concatenate([high, high, low], axis=1)
            results.append(jnp.dot(both, ops, preferred_element_type=F32))
        return results

    def state_gradients(m, g):
        size = (16, 48)[g]
        one, two = products_right(0, m, g, 128)
        for b in range(4):
            by_left = products_left(0, m, b, g, 2)
            for at, rows in places_of(g, b):
                for op in range(2):
                    grads[m, op, rows, :] = by_left[size * op + at : size * op + at + 8]
                at += size * b
                grads[m, 2, rows, :] = jnp.concatenate([one[at : at + 8], two[at : at + 8]], axis=1)

    def multiply(which, m, g):
        size = (16, 48)[g]
        by_right = products_right(which, m, g, 256)
        for b in range(4):
            by_left = products_left(which, m, b, g, 3)
            for at, rows in places_of(g, b):
                for op in range(3):
                    lhs_out[m, op, rows, :] = by_left[size * op + at : size * op + at + 8]
                at += size * b
                for h in range(2):
                    rhs_out[m, h, rows, :] = by_right[h][at : at + 8]

    def along_z(m, rows, kind):
        part = pl.ds(128 * kind, 128)
        return jnp.concatenate([rhs_out[m, 0, rows, part], rhs_out[m, 1, rows, part]], axis=1)

    def combine(vector, take, m, g, target):
        for p in GROUPS[g][2]:
            rows = rows_of(p)
            total = lhs_out[m, 2, rows, :] + along_z(m, rows, 1)
            total += state[0, rows, :] * lhs_out[m, 0, rows, :]
            total += state[1, rows, :] * lhs_out[m, 1, rows, :]
            total += state[2, rows, :] * along_z(m, rows, 0)
            for k in range(3):
                total += take(vector, k, rows) * grads[m, k, rows, :]
            put(target, m, rows, total * (plane[0] * float(WEIGHTS[p])))

    def apply_to_image(m):
        split_into(get, image, 1, m)
        for g in range(2):
            multiply(1, m, g)
            combine(image, get, m, g, local2)

    def send(turn, index, src, dst, peer):
        pltpu.make_async_remote_copy(
            src_ref=src,
            dst_ref=dst,
            send_sem=halo_send.at[turn, index],
            recv_sem=halo_recv.at[turn, index],
            device_id=peer,
            device_id_type=MESH,
        ).start()

    def send_x(turn, source, m):
        send(turn, 0, source.at[m, :, pl.ds(224, 32), :], recv_xl.at[turn, m], beside(1, 0))
        send(turn, 1, source.at[m, :, pl.ds(0, 32), :], recv_xh.at[turn, m], beside(-1, 0))

    def send_corners(turn, source):
        for m in range(3):
            for i, row in enumerate((0, 31, 224, 255)):
                send_c[turn, i, pl.ds(m, 1), :] = get(source, m, pl.ds(row, 1))
        for i, (dx, dy) in enumerate(((-1, -1), (-1, 1), (1, -1), (1, 1))):
            send(turn, 4 + i, send_c.at[turn, i], recv_c.at[turn, i], beside(dx, dy))

    def send_y(turn, source, m):
        send_yl[turn, m] = get(source, m, pl.ds(0, 8, stride=32))
        send_yh[turn, m] = get(source, m, pl.ds(31, 8, stride=32))
        send(turn, 2, send_yh.at[turn, m], recv_yl.at[turn, m], beside(0, 1))
        send(turn, 3, send_yl.at[turn, m], recv_yh.at[turn, m], beside(0, -1))

    def halo_refs(turn):
        refs = [recv_xl.at[turn], recv_xh.at[turn], recv_yl.at[turn], recv_yh.at[turn]]
        return refs + [recv_c.at[turn, i] for i in range(4)]

    def wait_halo(turn, sems):
        for i, ref in enumerate(halo_refs(turn)):
            pltpu.make_async_copy(ref, ref, sems.at[turn, i]).wait()

    def fold_y(target, first, count, stride):
        for m in range(3):
            for b in range(3):
                one = pl.ds(first + 8 * b + 7, count, stride=stride)
                two = pl.ds(first + 8 * b + 8, count, stride=stride)
                both = get(target, m, one) + get(target, m, two)
                put(target, m, one, both)
                put(target, m, two, both)

    def assemble_planes(turn, source, target):
        for m in range(3):
            value = get(source, m, rows_of(0)) + get(recv_xl.at[turn], m, pl.ds(0, 32))
            put(target, m, rows_of(0), fold_z(value * wall_xl))
            value = get(source, m, rows_of(7)) + get(recv_xh.at[turn], m, pl.ds(0, 32))
            put(target, m, rows_of(7), fold_z(value * wall_xh))
            at_m = pl.ds(m, 1)
            low = recv_yl[turn, m]
            low += jnp.where(row8 == 0, recv_c[turn, 3, at_m, :], 0.0)
            low += jnp.where(row8 == 7, recv_c[turn, 1, at_m, :], 0.0)
            high = recv_yh[turn, m]
            high += jnp.where(row8 == 0, recv_c[turn, 2, at_m, :], 0.0)
            high += jnp.where(row8 == 7, recv_c[turn, 0, at_m, :], 0.0)
            ysides[0, m] = fold_z(low) * wall_x
            ysides[1, m] = fold_z(high) * wall_x

    def assemble_sides(target):
        first, last = pl.ds(0, 8, stride=32), pl.ds(31, 8, stride=32)
        for m in range(3):
            put(target, m, first, (get(target, m, first) + ysides[0, m]) * wall_yl)
            put(target, m, last, (get(target, m, last) + ysides[1, m]) * wall_yh)

    def spread_out(phase, places, src_of, dst_of):
        for k, place in places:
            peer = peer_at(place)
            pltpu.make_async_remote_copy(
                src_ref=src_of(peer),
                dst_ref=dst_of(k),
                send_sem=red_send.at[phase],
                recv_sem=red_recv.at[phase],
                device_id=peer,
                device_id_type=MESH,
            ).start()

    def wait_bytes(ref, sem):
        pltpu.make_async_copy(ref, ref, sem).wait()

    loads[0].wait()
    loads[1].wait()
    for m in range(3):
        loads[2 + m].wait()
        split_into(whole, state, 0, m)
        state_gradients(m, 0)
    for m in range(3):
        loads[5 + m].wait()
        split_into(whole, direc, 1, m)
    for m in range(3):
        multiply(1, m, 0)
        combine(direc, whole, m, 0, local)
        if m == 0:
            pl.semaphore_wait(barrier, len(greeted))
        send_x(0, local, m)
    send_corners(0, local)
    loads[9].start()
    for m in range(3):
        state_gradients(m, 1)
        multiply(1, m, 1)
        combine(direc, whole, m, 1, local)
        send_y(0, local, m)
    for m in range(3):
        total = jnp.zeros((32, 256), F32)
        for p in range(1, 7):
            value = fold_z(get(local, m, rows_of(p)))
            put(image, m, rows_of(p), value)
            total += float(WEIGHTS[p]) * value
        tsum[m] = total
    fold_y(image, 32, 6, 32)

    loads[8].wait()
    elem = lax.broadcasted_iota(jnp.int32, (128, 1024), 0)
    spot = lax.broadcasted_iota(jnp.int32, (128, 1024), 1)
    wide = jnp.dot(
        jnp.broadcast_to(ids[...].astype(F32), (8, 128)).astype(BF16),
        (spot // 8 == elem).astype(F32).astype(BF16),
        preferred_element_type=F32,
    )
    for t in range(4):
        row = (lax.broadcasted_iota(jnp.int32, (8, 1024), 0) + 8 * t).astype(F32)
        onehot[pl.ds(8 * t, 8), :] = jnp.where(jnp.abs(wide - row) < 0.5, 1.0, 0.0)
    loads[9].wait()

    wait_halo(0, halo_recv)
    assemble_planes(0, local, image)

    weight8 = by_place(row8, weights4)
    y_next = ((row32 % 8 == 7) & (row32 != 31)).astype(F32)
    y_last = ((row32 % 8 == 0) & (row32 != 0)).astype(F32)
    wall_y = jnp.where(row32 == 0, wall_yl, jnp.where(row32 == 31, wall_yh, 1.0))
    coarse = []
    for m in range(3):
        total = tsum[m] + float(WEIGHTS[0]) * (get(image, m, rows_of(0)) + get(image, m, rows_of(7)))
        low, high = (
            jnp.sum(ysides[i, m] * weight8, axis=0, keepdims=True) for i in range(2)
        )
        total += jnp.where(row32 == 0, low, 0.0) + jnp.where(row32 == 31, high, 0.0)
        folded = total + pltpu.roll(total, 31, 0) * y_next + pltpu.roll(total, 1, 0) * y_last
        folded *= plane[0] * wall_y
        acc = jnp.zeros((32, 256), F32)
        for b in range(4):
            line = jnp.sum(folded[8 * b : 8 * b + 8], axis=0, keepdims=True)
            acc += onehot[:, pl.ds(256 * b, 256)] * line
        coarse.append(jnp.sum(acc, axis=1, keepdims=True))

    def form_part(slot, peer):
        chunk = lax.rem(peer[0], 4) * columns + peer[1]
        block = xxt[:, pl.ds(pl.multiple_of(chunk * 256, 256), 256)]
        for m in range(3):
            part_y[slot, pl.ds(m, 1), :] = jnp.sum(block * coarse[m], axis=0, keepdims=True)

    for k, place in in_plane:
        form_part(k, peer_at(place))
        spread_out(0, [(k, place)], lambda peer: part_y.at[k], lambda k: recv_y.at[k - 1])
    form_part(0, (gx, yz))
    assemble_sides(image)
    fold_y(image, 0, 2, 224)
    apply_to_image(0)
    wait_bytes(recv_y, red_recv.at[0])
    total = part_y[0]
    for k in range(PLANE - 1):
        total += recv_y[k]
    sum_b[...] = total
    spread_out(1, in_ring, lambda peer: sum_b, lambda k: recv_b.at[k - 1])
    apply_to_image(1)
    wait_bytes(recv_b, red_recv.at[1])
    total = sum_b[...]
    for k in range(RING - 1):
        total += recv_b[k]
    all_y[here] = total
    spread_out(2, in_plane, lambda peer: all_y.at[here], lambda k: all_y.at[here])
    apply_to_image(2)
    wait_bytes(all_y.at[pl.ds(0, PLANE - 1)], red_recv.at[2])

    sums = [jnp.zeros((32, 256), F32) for _ in range(3)]
    for j in range(PLANE):
        block = xxt[:, pl.ds(256 * j, 256)]
        for m in range(3):
            sums[m] += block * all_y[j, pl.ds(m, 1), :]
    for m in range(3):
        column = jnp.sum(sums[m], axis=1, keepdims=True)
        for b in range(4):
            line = jnp.sum(onehot[:, pl.ds(256 * b, 256)] * column, axis=0, keepdims=True)
            cblock[m, pl.ds(8 * b, 8), :] = jnp.broadcast_to(line, (8, 256))

    def add_correction(m, p):
        rows = rows_of(p)
        total = cblock[0] * grads[m, 0, rows, :]
        total += cblock[1] * grads[m, 1, rows, :]
        total += cblock[2] * grads[m, 2, rows, :]
        put(local2, m, rows, get(local2, m, rows) + total * (plane[0] * float(WEIGHTS[p])))

    for m in range(3):
        add_correction(m, 0)
        add_correction(m, 7)
        send_x(1, local2, m)
    send_corners(1, local2)
    for m in range(3):
        for p in range(1, 7):
            add_correction(m, p)
        send_y(1, local2, m)
    for m in range(3):
        for p in range(8):
            put(probe, m, rows_of(p), get(image, m, rows_of(p)) + cblock[m])

    def copies_out(source, target, n):
        copies = [
            pltpu.make_async_copy(
                source.at[:, h], target.at[:, :, pl.ds(128 * h, 128)], out_sem.at[n + h]
            )
            for h in range(2)
        ]
        for copy in copies:
            copy.start()
        return copies

    outs = copies_out(probe, probe_hbm, 0)
    for m in range(3):
        for p in range(1, 7):
            put(second, m, rows_of(p), fold_z(get(local2, m, rows_of(p))))

    def weighed(value, weights):
        return jnp.sum(jnp.sum(value * weights, axis=0, keepdims=True), axis=1, keepdims=True)

    inner = jnp.where((row32 % 8 == 0) | (row32 % 8 == 7), 0.0, plane[1])
    acc_in_sp, acc_in_pp, acc_pp = (jnp.zeros((32, 256), F32) for _ in range(3))
    for p in range(8):
        pp = jnp.zeros((32, 256), F32)
        for m in range(3):
            pr = get(probe, m, rows_of(p))
            pp += pr * pr
            if 0 < p < 7:
                acc_in_sp += get(second, m, rows_of(p)) * pr
        if 0 < p < 7:
            acc_in_pp += pp
        acc_pp += (0.5 if p in (0, 7) else 1.0) * pp
    in_sp, in_pp, pp = (
        weighed(acc_in_sp, inner),
        weighed(acc_in_pp, inner),
        weighed(acc_pp, plane[1]),
    )
    own = jnp.where(in_pp > 0, in_sp / jnp.where(in_pp > 0, in_pp, 1.0), 0.0)
    fold_y(second, 32, 6, 32)

    def residual_sums(places):
        q, rr = 0.0, 0.0
        for rows in places:
            for m in range(3):
                pr = get(probe, m, rows)
                rest = get(second, m, rows) - own * pr
                q += rest * pr
                rr += rest * rest
        return q, rr

    not_sides = jnp.where((row32 == 0) | (row32 == 31), 0.0, plane[1])
    sums_in = [v * not_sides for v in residual_sums([rows_of(p) for p in range(1, 7)])]

    wait_halo(1, halo_recv)
    assemble_planes(1, local2, second)
    assemble_sides(second)
    fold_y(second, 0, 2, 224)
    outs += copies_out(second, sec_hbm, 2)
    sums_faces = residual_sums([rows_of(0), rows_of(7)])
    sums_sides = residual_sums([pl.ds(32, 6, stride=32), pl.ds(63, 6, stride=32)])
    q, rr = (
        jnp.sum(
            jnp.sum(one + two * (0.5 * plane[1]), axis=0, keepdims=True)
            + jnp.sum(three, axis=0, keepdims=True) * plane[1, 0:1, :],
            axis=1,
            keepdims=True,
        )
        for one, two, three in zip(sums_in, sums_faces, sums_sides)
    )

    lane128 = lax.broadcasted_iota(jnp.int32, (1, 128), 1)

    def total_of(rows):
        return jnp.sum(rows, axis=0, keepdims=True)

    row_a[...] = jnp.where(
        lane128 < 32,
        own,
        jnp.where(lane128 < 64, q, jnp.where(lane128 < 96, pp, rr)),
    )
    spread_out(3, everyone, lambda peer: row_a, lambda k: recv_ra.at[pl.ds(k - 1, 1), :])
    recv_ra[pl.ds(255, 1), :] = row_a[...]
    wait_bytes(recv_ra.at[pl.ds(0, 255)], red_recv.at[3])
    own = recv_ra[...]
    q, pp, rr = (pltpu.roll(own, shift, 1) for shift in (96, 64, 32))
    weight_total = 343.0 * 128 * slabs * columns
    mean_sp, mean_pp = total_of(q + own * pp) / weight_total, total_of(pp) / weight_total
    coef = mean_sp / (mean_pp + epsilon)
    away = own - coef
    rest_mean = total_of(rr + 2.0 * away * q + away * away * pp) / weight_total
    rms = jnp.sqrt(jnp.maximum(rest_mean, 0.0) + epsilon)
    scal_ref[...] = jnp.concatenate([coef, rms, 1.0 / rms, jnp.zeros((5, 128), F32)], axis=0)

    wait_halo(0, halo_send)
    wait_halo(1, halo_send)
    wait_bytes(recv_y, red_send.at[0])
    wait_bytes(recv_b, red_send.at[1])
    wait_bytes(all_y.at[pl.ds(0, PLANE - 1)], red_send.at[2])
    wait_bytes(recv_ra.at[pl.ds(0, 255)], red_send.at[3])
    for out in outs:
        out.wait()


def normalise(second, probe, scal, basis_hbm, hess, basis, sems):
    coef, scale = scal[0:1, 0:1], scal[2:3, 0:1]
    hess[0] = scal[0, 0]
    hess[1] = scal[1, 0]
    stores = []
    for i in range(6):
        m, part = i // 2, pl.ds(128 * (i % 2), 128)
        for p in range(4):
            at = pl.ds(part.start + 32 * p, 32)
            basis[m, at, :] = (second[m, at, :] - coef * probe[m, at, :]) * scale
        stores.append(
            pltpu.make_async_copy(basis.at[m, part], basis_hbm.at[m, part], sems.at[i])
        )
        stores[-1].start()
    for store in stores:
        store.wait()


def shards(slabs, columns, state, direction, xxt_rows, coarse_ids):
    shape = state.shape
    ops = constants()
    vmem = pltpu.VMEM
    field = (3, 256, 256)
    halved = (3, 2, 256, 128)

    def body(*refs):
        kernel(slabs, columns, *refs)

    anywhere = pl.BlockSpec(memory_space=pl.ANY)
    sec, probe, scal = pl.pallas_call(
        body,
        out_shape=(
            jax.ShapeDtypeStruct(field, F32),
            jax.ShapeDtypeStruct(field, F32),
            jax.ShapeDtypeStruct((8, 128), F32),
        ),
        in_specs=[pl.BlockSpec(memory_space=pltpu.HBM)] * 5,
        out_specs=(anywhere, anywhere, pl.BlockSpec(memory_space=vmem)),
        scratch_shapes=[
            vmem(field, F32),
            vmem(field, F32),
            vmem((32, 8192), F32),
            vmem((1, 128), jnp.int32),
            vmem((192, 256), BF16),
            vmem((128, 512), BF16),
            vmem((2, 32, 256), F32),
            vmem((2, 3, 4, 64, 256), BF16),
            vmem((2, 3, 4, 64, 256), BF16),
            vmem((3, 3, 256, 256), F32),
            vmem((3, 3, 256, 256), F32),
            vmem((3, 2, 256, 256), F32),
            vmem(halved, F32),
            vmem(halved, F32),
            vmem(halved, F32),
            vmem(halved, F32),
            vmem(halved, F32),
            vmem((2, 3, 8, 256), F32),
            vmem((3, 32, 256), F32),
            vmem((32, 1024), F32),
            vmem((3, 32, 256), F32),
            vmem((PLANE, 4, 256), F32),
            vmem((PLANE - 1, 4, 256), F32),
            vmem((4, 256), F32),
            vmem((RING - 1, 4, 256), F32),
            vmem((PLANE, 4, 256), F32),
            vmem((2, 3, 8, 256), F32),
            vmem((2, 3, 8, 256), F32),
            vmem((2, 4, 4, 256), F32),
            vmem((2, 3, 2, 32, 128), F32),
            vmem((2, 3, 2, 32, 128), F32),
            vmem((2, 3, 8, 256), F32),
            vmem((2, 3, 8, 256), F32),
            vmem((2, 4, 4, 256), F32),
            vmem((1, 128), F32),
            vmem((256, 128), F32),
            pltpu.SemaphoreType.DMA((10,)),
            pltpu.SemaphoreType.DMA((4,)),
            pltpu.SemaphoreType.DMA((2, 8)),
            pltpu.SemaphoreType.DMA((2, 8)),
            pltpu.SemaphoreType.DMA((4,)),
            pltpu.SemaphoreType.DMA((4,)),
        ],
        compiler_params=pltpu.CompilerParams(
            collective_id=0, has_side_effects=True, vmem_limit_bytes=VMEM_LIMIT
        ),
        name="jacobian_products",
    )(
        state.reshape(field),
        direction.reshape(field),
        xxt_rows,
        coarse_ids,
        jnp.asarray(ops),
    )
    next_basis, hessenberg = pl.pallas_call(
        normalise,
        out_shape=(jax.ShapeDtypeStruct(field, F32), jax.ShapeDtypeStruct((2,), F32)),
        in_specs=[pl.BlockSpec(memory_space=vmem)] * 3,
        out_specs=(
            pl.BlockSpec(memory_space=pltpu.HBM),
            pl.BlockSpec(memory_space=pltpu.SMEM),
        ),
        scratch_shapes=[
            vmem(field, F32),
            pltpu.SemaphoreType.DMA((6,)),
        ],
        compiler_params=pltpu.CompilerParams(vmem_limit_bytes=16 * 1024 * 1024),
        name="normalise",
    )(sec, probe, scal)
    return next_basis.reshape(shape), hessenberg


def solution(mesh):
    slabs, columns = mesh.shape["gx"], mesh.shape["yz"]

    def local_shards(*args):
        return shards(slabs, columns, *args)

    return jax.shard_map(
        local_shards,
        mesh=mesh,
        in_specs=(
            P(None, "gx", "yz", None),
            P(None, "gx", "yz", None),
            P(("gx", "yz"), None),
            P(("gx", "yz"), None),
        ),
        out_specs=(P(None, "gx", "yz", None), P()),
        check_vma=False,
    )
```
